256 devices in a mesh: dp: 8 (over y, z_hi), seq: 32 (over z_lo, x, core).
Axes of the slice: x: 4, y: 4, z: 8 (z_hi: 2, z_lo: 4; z = z_hi * 4 + z_lo), core: 2. Of those that a mesh axis runs over, the one named last changes fastest.
Arguments:
- text_embed: bfloat16 [8, 4096, 4096], P('dp', 'seq'), may hold values from -6 to 6
- latents: bfloat16 [8, 256, 256], P('dp', 'seq'), may hold values from -6 to 6
- slot_order: int32 [8, 16], replicated, may hold values from 0 to 15, each once within a row
- conv_weight: bfloat16 [72, 256], replicated, may hold values from -0.75 to 0.75
- patch_weight: bfloat16 [1024, 4096], P(None, 'dp'), may hold values from -0.1875 to 0.1875
- norm_gain: float32 [4096], replicated, may hold values from 0.1 to 1.9
- query_weight: bfloat16 [4096, 2048], P(None, 'dp'), may hold values from -2.34375 to 2.34375
- key_weight: bfloat16 [4096, 2048], P(None, 'dp'), may hold values from -0.09375 to 0.09375
- value_weight: bfloat16 [4096, 2048], P(None, 'dp'), may hold values from -0.09375 to 0.09375
- out_weight: bfloat16 [2048, 4096], P('dp'), may hold values from -1 to 1
Outputs:
- attended: bfloat16 [8, 4096, 4096], P('dp', 'seq')
The draws below stay inside these ranges and needn't reach their ends.
Inputs may be any that keep to these rules, and one draw needn't show every extreme that they name: `slot_order`: each row holds every slot number once; only its first 8 entries place images.
All inputs are finite; a program needn't handle non-finite values.
Results may differ from the reference program's by a relative error of at most 0.025.
Values may be sent and summed in bfloat16 or wider, within the bound.
No kernel may reach another device: no remote copies, remote signals or barrier semaphores. Data moves between devices by JAX's collectives and lax.ppermute only.
A program may use at most 128 MiB of HBM per device.

```python
import jax
import jax.numpy as jnp
from jax import lax

D = 4096
HEADSZ = 128
HEADS = 16
UCH = 256
LAT_SIDE = 32
LAT_C = 8
IMG_TOK = 256
SEQS = 8
SEQ_LEN = 4096
SLOTS = 16
IMGS = 8
N_DP = 8


def shared_base(key):
    return jnp.clip(jax.random.normal(key, (D, HEADS * HEADSZ), jnp.float32), -6.0, 6.0)


def draw_key_weight(key, part):
    base = shared_base(key)
    return (base * D ** (-0.5)).astype(jnp.bfloat16)


def draw_query_weight(key, part):
    key = jax.random.fold_in(key, 12)
    first = jax.random.fold_in(key, 0)
    noise = jnp.clip(jax.random.normal(first, (D, HEADS * HEADSZ), jnp.float32), -6.0, 6.0) * (D // 4) ** (-0.5)
    return noise.astype(jnp.bfloat16)


def draw_text_embed(key, part):
    key = jax.random.fold_in(key, 21)
    first = jax.random.fold_in(key, 0)
    return jnp.clip(jax.random.normal(first, (SEQS, SEQ_LEN, D), jnp.float32), -6.0, 6.0).astype(jnp.bfloat16)


def steps_of(stream_key, shape, shards, least, largest):
    level, own = 1.0, jax.random.fold_in(stream_key, 6)
    for position, shards_of in shards:
        heights = jnp.exp(jax.random.uniform(jax.random.fold_in(own, position), (shards_of,), jnp.float32, least / len(shards), largest / len(shards)))
        level = level * jnp.repeat(heights, shape[position] // shards_of).reshape([-1 if axis == position else 1 for axis in range(len(shape))])
    return level


def gaussian(own_key, extent, width, reach, cuts=(), held_as=jnp.bfloat16):
    drawn = width * jax.random.normal(own_key, extent, jnp.float32)
    if cuts:
        drawn = drawn * steps_of(own_key, extent, cuts, -0.22, 0.18)
    return jnp.clip(drawn, -reach, reach).astype(held_as)


def setup_inputs(seed: int = 0) -> dict:
    key_of = jax.random.split(jax.random.key(seed), 11)
    text_embed = draw_text_embed(jax.random.fold_in(key_of[10], 71), 0)
    latents = gaussian(key_of[1], (SEQS, IMGS * LAT_SIDE, LAT_SIDE * LAT_C), 1.0, 6.0, ((0, 8), (1, 32)))
    slot_order = jax.vmap(lambda own: jax.random.permutation(own, SLOTS))(jax.random.split(key_of[2], SEQS)).reshape((SEQS, SLOTS)).astype(jnp.int32)
    conv_weight = gaussian(key_of[3], (9 * LAT_C, UCH), (9 * LAT_C) ** -0.5, 0.75)
    patch_weight = gaussian(key_of[4], (4 * UCH, D), (4 * UCH) ** -0.5, 0.1875, ((1, 8),))
    norm_gain = jnp.clip(1.0 + 0.18 * jax.random.normal(key_of[5], (D,), jnp.float32), 0.1, 1.9)
    query_weight = draw_query_weight(jax.random.fold_in(key_of[10], 71), 0)
    key_weight = draw_key_weight(jax.random.fold_in(key_of[10], 71), 0)
    value_weight = gaussian(key_of[8], (D, HEADS * HEADSZ), D ** -0.5, 0.09375, ((1, 8),))
    out_weight = gaussian(key_of[9], (HEADS * HEADSZ, D), (HEADS * HEADSZ // 64) ** -0.5, 1.0, ((0, 8),))
    return {"text_embed": text_embed, "latents": latents, "slot_order": slot_order, "conv_weight": conv_weight, "patch_weight": patch_weight, "norm_gain": norm_gain, "query_weight": query_weight, "key_weight": key_weight, "value_weight": value_weight, "out_weight": out_weight}


def conv_rows(padded, row_ids, conv_weight):
    row_count = row_ids.shape[0]
    image_row = row_ids % LAT_SIDE
    above_rows = padded[0:row_count] * (image_row != 0)[:, None].astype(padded.dtype)
    middle = padded[1:row_count + 1]
    below_rows = padded[2:row_count + 2] * (image_row != LAT_SIDE - 1)[:, None].astype(padded.dtype)
    tap_list = []
    for row_block in (above_rows, middle, below_rows):
        shaped = row_block.reshape(row_count, LAT_SIDE, LAT_C)
        widened = jnp.pad(shaped, ((0, 0), (1, 1), (0, 0)))
        for offset_col in range(3):
            tap_list.append(widened[:, offset_col:offset_col + LAT_SIDE, :])
    stacked = jnp.stack(tap_list, axis=2).reshape(row_count * LAT_SIDE, 9 * LAT_C)
    feature = jnp.dot(stacked, conv_weight, preferred_element_type=jnp.float32)
    feature = jax.nn.silu(feature)
    channels = feature.shape[-1]
    feature = feature.reshape(row_count // 2, 2, LAT_SIDE // 2, 2, channels)
    feature = feature.transpose(0, 2, 1, 3, 4).reshape(row_count // 2 * (LAT_SIDE // 2), 4 * channels)
    return feature.astype(jnp.bfloat16)

def image_numbers(positions, slot_row, images_count):
    slot_ids = positions // IMG_TOK
    matches = slot_ids[:, None] == slot_row[None, :images_count]
    numbers = jnp.arange(images_count, dtype=jnp.int32)[None, :] + 1
    return lax.optimization_barrier(jnp.sum(jnp.where(matches, numbers, 0), axis=1)).astype(jnp.int32) - 1

def attend_block(query_block, query_place, query_image, key_rows, value_rows, key_place, key_image):
    scores = jnp.einsum('qd,kd->qk', query_block.astype(jnp.float32), key_rows.astype(jnp.float32)) * HEADSZ ** (-0.5)
    allowed = (key_place[None, :] <= query_place[:, None]) | (key_image[None, :] == query_image[:, None]) & (query_image[:, None] >= 0)
    row_top = lax.optimization_barrier(jnp.max(jnp.where(allowed, scores, -jnp.inf), axis=1, keepdims=True))
    weights = jnp.where(allowed, jnp.exp(scores - row_top), jnp.float32(0.0))
    shares = (weights / lax.optimization_barrier(jnp.sum(weights, axis=1, keepdims=True))).astype(jnp.bfloat16)
    return jnp.dot(shares, value_rows, preferred_element_type=jnp.float32).astype(jnp.bfloat16)

def reference(text_embed, latents, slot_order, conv_weight, patch_weight, norm_gain, query_weight, key_weight, value_weight, out_weight):
    outputs = []
    places = jnp.arange(SEQ_LEN, dtype=jnp.int32)
    block_size = min(512, SEQ_LEN)
    blocks = SEQ_LEN // block_size
    group_width = HEADS // N_DP * HEADSZ
    for sequence in range(SEQS):
        lat_rows = jnp.roll(latents[sequence], LAT_SIDE // 2, axis=0)
        padded = jnp.pad(lat_rows, ((1, 1), (0, 0)))
        features = conv_rows(padded, jnp.arange(lat_rows.shape[0], dtype=jnp.int32), conv_weight)
        embedded = jnp.dot(features, patch_weight, preferred_element_type=jnp.float32).astype(jnp.bfloat16)
        image_ids = image_numbers(places, slot_order[sequence], IMGS)
        source = (jnp.maximum(image_ids, 0) * IMG_TOK + places % IMG_TOK).astype(jnp.int32)
        joint_rows = jnp.where((image_ids >= 0)[:, None], jnp.take(embedded, source, axis=0), text_embed[sequence])
        widened = joint_rows.astype(jnp.float32)
        normed = (widened * lax.rsqrt(lax.optimization_barrier(jnp.mean(widened * widened, axis=1, keepdims=True)) + 1e-05) * norm_gain).astype(jnp.bfloat16)
        queries = jnp.dot(normed, query_weight, preferred_element_type=jnp.float32).astype(jnp.bfloat16)
        key_rows = jnp.dot(normed, key_weight, preferred_element_type=jnp.float32).astype(jnp.bfloat16)
        value_rows = jnp.dot(normed, value_weight, preferred_element_type=jnp.float32).astype(jnp.bfloat16)
        queries = queries.reshape(SEQ_LEN, HEADS, HEADSZ).transpose(1, 0, 2)
        key_rows = key_rows.reshape(SEQ_LEN, HEADS, HEADSZ).transpose(1, 0, 2)
        value_rows = value_rows.reshape(SEQ_LEN, HEADS, HEADSZ).transpose(1, 0, 2)

        def one_head(inputs):
            head_query, head_key, head_value = inputs

            def one_block(block_inputs):
                return attend_block(block_inputs[0], block_inputs[1], block_inputs[2], head_key, head_value, places, image_ids)
            done = lax.map(one_block, (head_query.reshape(blocks, block_size, HEADSZ), places.reshape(blocks, block_size), image_ids.reshape(blocks, block_size)))
            return done.reshape(SEQ_LEN, HEADSZ)
        heads_out = lax.map(one_head, (queries, key_rows, value_rows))
        head_outputs = heads_out.transpose(1, 0, 2).reshape(SEQ_LEN, HEADS * HEADSZ)
        totals = jnp.zeros((SEQ_LEN, D), jnp.float32)
        for member in range(N_DP):
            group_part = jnp.dot(head_outputs[:, member * group_width:(member + 1) * group_width], out_weight[member * group_width:(member + 1) * group_width], preferred_element_type=jnp.float32).astype(jnp.bfloat16)
            totals = totals + group_part.astype(jnp.float32)
        outputs.append(totals.astype(jnp.bfloat16))
    return jnp.stack(outputs)
```

```python
import functools
import math

import jax
import jax.numpy as jnp
import numpy as np
from jax import lax
from jax.experimental import pallas as pl
from jax.experimental.pallas import tpu as pltpu
from jax.sharding import Mesh, PartitionSpec as P

HEADSZ = 128
LAT_SIDE = 32
LAT_C = 8
IMG_TOK = 256
N_Y, N_ZH, N_ZL, N_X, N_C = 4, 2, 4, 4, 2
ROWS = 128
SLOTS = 16
IMGS = 8
D = 4096
EXP2_SCALE = HEADSZ**-0.5 * math.log2(math.e)


def shift(value, axis, size, step):
    return lax.ppermute(value, axis, [((i + step) % size, i) for i in range(size)])


def ring(value, axis):
    after = shift(value, axis, 4, 1)
    before = shift(value, axis, 4, 3)
    across = shift(value, axis, 4, 2)
    return [value, after, across, before]


def place(blocks, index, axis):
    length = blocks[0].shape[axis]
    shape = list(blocks[0].shape)
    shape[axis] = length * len(blocks)
    whole = jnp.zeros(shape, blocks[0].dtype)
    for step, block in enumerate(blocks):
        start = ((index + step) % len(blocks)) * length
        whole = lax.dynamic_update_slice_in_dim(whole, block, start, axis)
    return whole


def features_of(rows, conv_weight):
    count = rows.shape[0]
    taps = []
    for row in range(3):
        shaped = rows[:, row : row + 16].reshape(count, 16, LAT_SIDE, LAT_C)
        widened = jnp.pad(shaped, ((0, 0), (0, 0), (1, 1), (0, 0)))
        for col in range(3):
            taps.append(widened[:, :, col : col + LAT_SIDE])
    stacked = jnp.stack(taps, axis=3).reshape(count * 16 * LAT_SIDE, 9 * LAT_C)
    feature = jnp.dot(stacked, conv_weight, preferred_element_type=jnp.float32)
    feature = jax.nn.silu(feature).astype(jnp.bfloat16)
    feature = feature.reshape(count, 8, 2, 16, 2, feature.shape[-1])
    return feature.transpose(0, 1, 3, 2, 4, 5).reshape(count * ROWS, -1)


def attend_kernel(flags, own, other, out, scores):
    block = pl.program_id(0)
    core = flags[SLOTS]
    query = own[pl.ds(2 * block, 2), :, 0:128].reshape(256, 128)

    def chunk(ref, index, first):
        return ref[pl.ds(2 * index, 2), :, first : first + 128].reshape(256, 128)

    def dots(key):
        return lax.dot_general(
            query, key, (((1,), (1,)), ((), ())), preferred_element_type=jnp.float32
        )

    def halves(index):
        return dots(chunk(own, index, 128)), dots(chunk(other, index, 0))

    def top(value, mx):
        return jnp.maximum(mx, jnp.maximum(value[:, :128], value[:, 128:]))

    def first_pass(index, mx):
        mine, theirs = halves(index)
        start = pl.multiple_of(index * 512, 512)
        scores[:, pl.ds(start, 256)] = mine
        scores[:, pl.ds(start + 256, 256)] = theirs
        return top(theirs, top(mine, mx))

    mx = lax.fori_loop(0, block, first_pass, jnp.full((256, 128), -jnp.inf, jnp.float32))
    mine, theirs = halves(block)
    q_id = lax.broadcasted_iota(jnp.int32, (256, 256), 0)
    k_id = lax.broadcasted_iota(jnp.int32, (256, 256), 1)
    q_slot, k_slot = q_id // 128, k_id // 128
    image = jnp.where(q_slot == 0, flags[2 * block], flags[2 * block + 1]) > 0
    same = q_slot == k_slot
    earlier = k_slot < q_slot
    mine_ok = earlier | (same & ((k_id <= q_id) | image))
    theirs_ok = earlier | (same & (image | (core == 1)))
    mine = jnp.where(mine_ok, mine, -jnp.inf)
    theirs = jnp.where(theirs_ok, theirs, -jnp.inf)
    last = pl.multiple_of(block * 512, 512)
    scores[:, pl.ds(last, 256)] = mine
    scores[:, pl.ds(last + 256, 256)] = theirs
    mx = top(theirs, top(mine, mx))
    limit = jnp.max(mx, axis=1, keepdims=True) * EXP2_SCALE

    def second_pass(index, carry):
        total, acc = carry
        start = pl.multiple_of(index * 512, 512)
        mine = jnp.exp2(scores[:, pl.ds(start, 256)] * EXP2_SCALE - limit)
        theirs = jnp.exp2(scores[:, pl.ds(start + 256, 256)] * EXP2_SCALE - limit)
        total = total + (mine[:, :128] + mine[:, 128:]) + (theirs[:, :128] + theirs[:, 128:])
        acc = acc + jnp.dot(
            mine.astype(jnp.bfloat16), chunk(own, index, 256), preferred_element_type=jnp.float32
        )
        acc = acc + jnp.dot(
            theirs.astype(jnp.bfloat16), chunk(other, index, 128), preferred_element_type=jnp.float32
        )
        return total, acc

    zero = jnp.zeros((256, 128), jnp.float32)
    total, acc = lax.fori_loop(0, block + 1, second_pass, (zero, zero))
    total = jnp.sum(total, axis=1, keepdims=True)
    out[...] = (acc / total).astype(jnp.bfloat16).reshape(2, 128, 128)


def attend(flags, own, other):
    return pl.pallas_call(
        attend_kernel,
        out_shape=jax.ShapeDtypeStruct((SLOTS, ROWS, HEADSZ), jnp.bfloat16),
        grid_spec=pltpu.PrefetchScalarGridSpec(
            num_scalar_prefetch=1,
            grid=(SLOTS // 2,),
            in_specs=[
                pl.BlockSpec((SLOTS, ROWS, 3 * HEADSZ), lambda i, s: (0, 0, 0)),
                pl.BlockSpec((SLOTS, ROWS, 2 * HEADSZ), lambda i, s: (0, 0, 0)),
            ],
            out_specs=pl.BlockSpec((2, ROWS, HEADSZ), lambda i, s: (i, 0, 0)),
            scratch_shapes=[pltpu.VMEM((256, 4096), jnp.float32)],
        ),
        compiler_params=pltpu.CompilerParams(vmem_limit_bytes=32 * 1024 * 1024),
        cost_estimate=pl.CostEstimate(
            flops=4 * 36 * 256 * 512 * 128, bytes_accessed=3 << 20, transcendentals=36 * 256 * 512
        ),
    )(flags, own, other)


def shards(
    text_embed,
    latents,
    slot_order,
    conv_weight,
    patch_weight,
    norm_gain,
    query_weight,
    key_weight,
    value_weight,
    out_weight,
):
    y, zh, zl, x, c = (lax.axis_index(name) for name in ("y", "zh", "zl", "x", "c"))
    slot = zl * N_X + x
    piece = c * N_X + x

    texts = ring(text_embed[0], "y")

    qkv_own = jnp.concatenate([query_weight, key_weight, value_weight], axis=1)
    qkv_piece = lax.dynamic_slice_in_dim(qkv_own, piece * 512, 512, 0)
    qkv_piece = shift(qkv_piece, "zh", N_ZH, 1)
    qkv_half = place(ring(qkv_piece, "x"), x, 0)
    qkv_far = place([qkv_half, shift(qkv_half, "c", N_C, 1)], c, 0)

    patch_piece = lax.dynamic_slice_in_dim(patch_weight, piece * 128, 128, 0)
    patch_piece = place([patch_piece, shift(patch_piece, "zh", N_ZH, 1)], zh, 1)
    patch_piece = place(ring(patch_piece, "y"), y, 1)
    patch_half = place(ring(patch_piece, "x"), x, 0)
    patch_all = place([patch_half, shift(patch_half, "c", N_C, 1)], c, 0)

    spread = jnp.broadcast_to(latents, (N_ZL * N_X * N_C, 8, LAT_SIDE * LAT_C))
    lat_rows = lax.all_to_all(spread, ("zl", "x", "c"), split_axis=0, concat_axis=0, tiled=True)
    lat_rows = lat_rows.reshape(-1, LAT_SIDE * LAT_C)
    dp = y * N_ZH + zh
    slot_row = lax.dynamic_slice_in_dim(slot_order, dp, 1, 0)[0]
    image = jnp.sum(jnp.where(slot_row[:IMGS] == slot, jnp.arange(IMGS, dtype=jnp.int32), 0))
    first = (image * LAT_SIDE + c * 16 - 17) % (IMGS * LAT_SIDE)
    lat_rows = jnp.concatenate([lat_rows, lat_rows[:32]], axis=0)
    picked = lax.dynamic_slice_in_dim(lat_rows, first, 18, 0)
    row_id = jnp.arange(18)
    inside = ((row_id != 0) | (c != 0)) & ((row_id != 17) | (c != 1))
    picked = jnp.where(inside[:, None], picked, jnp.zeros_like(picked))
    features = features_of(jnp.stack(ring(picked, "y")), conv_weight)
    embedded = jnp.dot(features, patch_all, preferred_element_type=jnp.float32)
    embedded = embedded.astype(jnp.bfloat16).reshape(N_Y, ROWS, D)

    joint = []
    for step in range(N_Y):
        seq = ((y + step) % N_Y) * N_ZH + zh
        row = lax.dynamic_slice_in_dim(slot_order, seq, 1, 0)[0]
        is_image = jnp.any(row[:IMGS] == slot)
        joint.append(jnp.where(is_image, embedded[step], texts[step]))
    joint = jnp.concatenate(joint, axis=0)
    widened = joint.astype(jnp.float32)
    scale = lax.rsqrt(jnp.mean(widened * widened, axis=1, keepdims=True) + 1e-05)
    normed = (widened * scale * norm_gain).astype(jnp.bfloat16)

    near = jnp.dot(normed, qkv_own, preferred_element_type=jnp.float32).astype(jnp.bfloat16)
    far = jnp.dot(normed, qkv_far, preferred_element_type=jnp.float32).astype(jnp.bfloat16)
    joined = jnp.stack([near, far]).reshape(2, N_Y, ROWS, 3, 2, HEADSZ)
    blocks = joined.transpose(1, 0, 4, 2, 3, 5).reshape(SLOTS, ROWS, 3 * HEADSZ)
    own = lax.all_to_all(blocks, ("zl", "x"), split_axis=0, concat_axis=0, tiled=True)
    other = shift(own[:, :, HEADSZ:], "c", N_C, 1)

    seq = ((y + zl) % N_Y) * N_ZH + zh
    row = lax.dynamic_slice_in_dim(slot_order, seq, 1, 0)[0]
    is_image = jnp.any(row[None, :IMGS] == jnp.arange(SLOTS)[:, None], axis=1)
    flags = jnp.concatenate([is_image.astype(jnp.int32), c[None].astype(jnp.int32)])
    heads = attend(flags, own, other)

    moves = [
        (((a * N_ZL) + b), (((a + b) % N_Y) * N_ZL + b)) for a in range(N_Y) for b in range(N_ZL)
    ]
    heads = lax.ppermute(heads, ("y", "zl"), moves)
    heads = lax.all_to_all(heads, ("zl", "x"), split_axis=0, concat_axis=0, tiled=True)
    merged = heads.transpose(1, 0, 2).reshape(ROWS, SLOTS * HEADSZ)

    out_piece = lax.dynamic_slice_in_dim(out_weight, piece * 512, 512, 1)
    out_piece = jnp.concatenate([out_piece, shift(out_piece, "zh", N_ZH, 1)], axis=0)
    own_y, after, across, before = ring(out_piece, "y")
    out_piece = jnp.concatenate([own_y, before, across, after], axis=0)
    near_cols = ring(out_piece, "x")
    near_cols = place(near_cols, x, 1)
    far_cols = shift(near_cols, "c", N_C, 1)
    result = place(
        [
            jnp.dot(merged, part, preferred_element_type=jnp.float32).astype(jnp.bfloat16)
            for part in (near_cols, far_cols)
        ],
        c,
        1,
    )
    return result[None]


def solution(mesh):
    fine = Mesh(
        np.asarray(mesh.devices).reshape(N_Y, N_ZH, N_ZL, N_X, N_C), ("y", "zh", "zl", "x", "c")
    )
    dp, seq = ("y", "zh"), ("zl", "x", "c")
    return jax.shard_map(
        shards,
        mesh=fine,
        in_specs=(
            P(dp, seq, None),
            P(dp, seq, None),
            P(),
            P(),
            P(None, dp),
            P(),
            P(None, dp),
            P(None, dp),
            P(None, dp),
            P(dp, None),
        ),
        out_specs=P(dp, seq, None),
        check_vma=False,
    )
```

```python
import functools
import math

import jax
import jax.numpy as jnp
import numpy as np
from jax import lax
from jax.experimental import pallas as pl
from jax.experimental.pallas import tpu as pltpu
from jax.sharding import Mesh, PartitionSpec as P

HEADSZ = 128
LAT_SIDE = 32
LAT_C = 8
IMG_TOK = 256
N_Y, N_ZH, N_ZL, N_X, N_C = 4, 2, 4, 4, 2
ROWS = 128
SLOTS = 16
IMGS = 8
D = 4096
EXP2_SCALE = HEADSZ**-0.5 * math.log2(math.e)


def shift(value, axis, size, step):
    return lax.ppermute(value, axis, [((i + step) % size, i) for i in range(size)])


def ring(value, axis):
    after = shift(value, axis, 4, 1)
    before = shift(value, axis, 4, 3)
    across = shift(value, axis, 4, 2)
    return [value, after, across, before]


def place(blocks, index, axis):
    length = blocks[0].shape[axis]
    shape = list(blocks[0].shape)
    shape[axis] = length * len(blocks)
    whole = jnp.zeros(shape, blocks[0].dtype)
    for step, block in enumerate(blocks):
        start = ((index + step) % len(blocks)) * length
        whole = lax.dynamic_update_slice_in_dim(whole, block, start, axis)
    return whole


def patch_matrix(conv_weight):
    taps = conv_weight.reshape(3, 3, LAT_C, -1)
    cells = [
        jnp.pad(taps, ((i, 1 - i), (j, 1 - j), (0, 0), (0, 0))) for i in range(2) for j in range(2)
    ]
    return jnp.stack(cells, axis=3).reshape(16 * LAT_C, -1)


def features_of(rows, conv_weight):
    count = rows.shape[0]
    padded = jnp.pad(rows, ((0, 0), (0, 0), (LAT_C, LAT_C)))
    pairs = padded.reshape(count, 18, 17, 2 * LAT_C)
    parts = []
    for row in range(4):
        line = pairs[:, row : row + 15 : 2]
        parts += [line[:, :, :16], line[:, :, 1:]]
    windows = jnp.concatenate(parts, axis=3).reshape(count * ROWS, 16 * LAT_C)
    feature = jnp.dot(
        windows, patch_matrix(conv_weight), preferred_element_type=jnp.float32
    )
    return jax.nn.silu(feature).astype(jnp.bfloat16)


def project_kernel(flags, base, rows, features, inverse, *refs):
    weights, folded, out, total = refs[:3], refs[3:6], refs[6], refs[7]
    step = pl.program_id(0)

    @pl.when(step == 0)
    def _():
        total[...] = jnp.zeros_like(total)

    for part in range(3):
        cols = slice(part * 256, part * 256 + 256)
        total[:, cols] += jnp.dot(
            rows[...], weights[part][...], preferred_element_type=jnp.float32
        )

    @pl.when(step == pl.num_programs(0) - 1)
    def _():
        for part in range(3):
            cols = slice(part * 256, part * 256 + 256)
            image = jnp.dot(features[...], folded[part][...], preferred_element_type=jnp.float32)
            image = image * inverse[...]
            for seq in range(N_Y):
                some = slice(seq * ROWS, seq * ROWS + ROWS)
                kept = jnp.where(flags[seq] > 0, image[some], total[some, cols])
                kept = kept.astype(jnp.bfloat16)
                for head in range(2):
                    out[seq, head, :, part * HEADSZ : part * HEADSZ + HEADSZ] = kept[
                        :, head * HEADSZ : head * HEADSZ + HEADSZ
                    ]


def project(flags, base, rows, features, inverse, weights, folded, half):
    depth = 512
    if len(weights) == 3:
        weight_specs = [pl.BlockSpec((depth, 256), lambda i, s: (i, 0))] * 3
    else:
        weights = list(weights) * 3
        weight_specs = [
            pl.BlockSpec((depth, 256), functools.partial(lambda p, i, s: (i, p), p))
            for p in range(3)
        ]
    folded_specs = [
        pl.BlockSpec((1024, 256), functools.partial(lambda p, i, s: (0, p), 3 * half + p))
        for p in range(3)
    ]
    aliases = {}
    if base is None:
        base = jnp.zeros((8, 128), jnp.bfloat16)
    else:
        aliases = {1: 0}
    return pl.pallas_call(
        project_kernel,
        out_shape=jax.ShapeDtypeStruct((N_Y, 4, ROWS, 3 * HEADSZ), jnp.bfloat16),
        grid_spec=pltpu.PrefetchScalarGridSpec(
            num_scalar_prefetch=1,
            grid=(D // depth,),
            in_specs=[
                pl.BlockSpec(memory_space=pl.ANY),
                pl.BlockSpec((N_Y * ROWS, depth), lambda i, s: (0, i)),
                pl.BlockSpec((N_Y * ROWS, 1024), lambda i, s: (0, 0)),
                pl.BlockSpec((N_Y * ROWS, 1), lambda i, s: (0, 0)),
                *weight_specs,
                *folded_specs,
            ],
            out_specs=pl.BlockSpec((N_Y, 2, ROWS, 3 * HEADSZ), lambda i, s: (0, half, 0, 0)),
            scratch_shapes=[pltpu.VMEM((N_Y * ROWS, 768), jnp.float32)],
        ),
        input_output_aliases=aliases,
        compiler_params=pltpu.CompilerParams(vmem_limit_bytes=40 * 1024 * 1024),
        cost_estimate=pl.CostEstimate(
            flops=2 * 512 * 5120 * 768, bytes_accessed=12 << 20, transcendentals=0
        ),
    )(flags, base, rows, features, inverse, *weights, *[folded] * 3)


def output_kernel(core, *refs):
    heads, parts, out = refs[:4], refs[4:8], refs[8]
    block = pl.program_id(0)
    for part in range(4):

        @pl.when(block // 4 == part)
        def _(part=part):
            total = jnp.zeros(out.shape, jnp.float32)
            for step in range(N_Y):
                weight = parts[part][step]
                for head in range(4):
                    total = total + jnp.dot(
                        heads[step][head],
                        weight[head * HEADSZ : head * HEADSZ + HEADSZ],
                        preferred_element_type=jnp.float32,
                    )
            out[...] = total.astype(out.dtype)


def output(core, heads, parts):
    def weight_map(part, i, s):
        return 0, 0, jnp.clip(i - 4 * part, 0, 3)

    def out_map(i, s):
        return 0, i % 8 + 8 * jnp.where(i < 8, s[0], 1 - s[0])

    return pl.pallas_call(
        output_kernel,
        out_shape=jax.ShapeDtypeStruct((ROWS, D), jnp.bfloat16),
        grid_spec=pltpu.PrefetchScalarGridSpec(
            num_scalar_prefetch=1,
            grid=(16,),
            in_specs=[pl.BlockSpec((4, ROWS, HEADSZ), lambda i, s: (0, 0, 0))] * 4
            + [
                pl.BlockSpec((N_Y, 512, 256), functools.partial(weight_map, part))
                for part in range(4)
            ],
            out_specs=pl.BlockSpec((ROWS, 256), out_map),
        ),
        compiler_params=pltpu.CompilerParams(vmem_limit_bytes=40 * 1024 * 1024),
        cost_estimate=pl.CostEstimate(
            flops=2 * 128 * 2048 * 4096, bytes_accessed=18 << 20, transcendentals=0
        ),
    )(core, *heads, *parts)


def is_image(slot_order, seq, slot):
    row = lax.dynamic_slice_in_dim(slot_order, seq, 1, 0)[0]
    return jnp.any(row[None, :IMGS] == slot[:, None], axis=1).astype(jnp.int32)


def shards(
    text_embed,
    latents,
    slot_order,
    conv_weight,
    patch_weight,
    norm_gain,
    query_weight,
    key_weight,
    value_weight,
    out_weight,
):
    y, zh, zl, x, c = (lax.axis_index(name) for name in ("y", "zh", "zl", "x", "c"))
    slot = zl * N_X + x
    own_weights = (query_weight, key_weight, value_weight)
    sync = lax.optimization_barrier

    def normed_rows(value):
        widened = value.astype(jnp.float32)
        scale = lax.rsqrt(jnp.mean(widened * widened, axis=1, keepdims=True) + 1e-05)
        return (widened * scale * norm_gain).astype(jnp.bfloat16)

    texts = [text_embed[0], None, None, None]
    texts[1] = shift(texts[0], "y", N_Y, 1)
    texts[3] = shift(texts[0], "y", N_Y, 3)

    first = c * 512 + zl * 128 + x * 32
    patch_rows = lax.dynamic_slice_in_dim(patch_weight, first, 32, 0)
    patch_rows = place([patch_rows, shift(patch_rows, "zh", N_ZH, 1)], zh, 1)
    patch_rows = place(ring(patch_rows, "y"), y, 1)
    gained = (patch_rows.astype(jnp.float32) * norm_gain).astype(jnp.bfloat16)
    folded = jnp.concatenate(
        [
            jnp.dot(gained, weight, preferred_element_type=jnp.float32).astype(jnp.bfloat16)
            for weight in own_weights
        ],
        axis=1,
    )
    folded = jnp.concatenate([folded, shift(folded, "zh", N_ZH, 1)], axis=1)

    first = c * 2048 + x * 512 + zl * 128
    far = jnp.concatenate(
        [lax.dynamic_slice_in_dim(weight, first, 128, 0) for weight in own_weights], axis=1
    )
    far = shift(far, "zh", N_ZH, 1)
    far = place(ring(far, "zl"), zl, 0)

    spread = jnp.broadcast_to(latents, (N_ZL * N_X * N_C, 8, LAT_SIDE * LAT_C))
    lat_rows = lax.all_to_all(spread, ("zl", "x", "c"), split_axis=0, concat_axis=0, tiled=True)
    lat_rows = lat_rows.reshape(-1, LAT_SIDE * LAT_C)
    slot_row = lax.dynamic_slice_in_dim(slot_order, y * N_ZH + zh, 1, 0)[0]
    image = jnp.sum(jnp.where(slot_row[:IMGS] == slot, jnp.arange(IMGS, dtype=jnp.int32), 0))
    first = (image * LAT_SIDE + c * 16 - 17) % (IMGS * LAT_SIDE)
    lat_rows = jnp.concatenate([lat_rows, lat_rows[:32]], axis=0)
    picked = lax.dynamic_slice_in_dim(lat_rows, first, 18, 0)
    row_id = jnp.arange(18)
    inside = ((row_id != 0) | (c != 0)) & ((row_id != 17) | (c != 1))
    picked = jnp.where(inside[:, None], picked, jnp.zeros_like(picked))
    picked = jnp.stack([picked, shift(picked, "zh", N_ZH, 1)])
    picked = jnp.stack(ring(picked, "y"), axis=1)

    texts[0], texts[1], texts[3], folded, far, picked = sync(
        (texts[0], texts[1], texts[3], folded, far, picked)
    )
    texts[2] = shift(texts[0], "y", N_Y, 2)
    folded = place(ring(folded, "x"), x, 0)
    folded = place(ring(folded, "zl"), zl, 0)
    far = place(ring(far, "x"), x, 0)
    features = features_of(picked.reshape(2 * N_Y, 18, LAT_SIDE * LAT_C), conv_weight)
    embedded = jnp.dot(features, patch_weight, preferred_element_type=jnp.float32)
    squares = jnp.sum(embedded * embedded, axis=1).reshape(2, N_Y, ROWS)
    squares = squares[0] + shift(squares[1], "zh", N_ZH, 1)
    squares = sum(jnp.roll(part, step, axis=0) for step, part in enumerate(ring(squares, "y")))
    inverse = lax.rsqrt(squares.reshape(N_Y * ROWS, 1) / D + 1e-05)
    piece = lax.dynamic_slice_in_dim(out_weight, c * 2048 + x * 256, 256, 1)
    piece = jnp.concatenate(
        [piece, lax.dynamic_slice_in_dim(out_weight, c * 2048 + 1024 + x * 256, 256, 1)], axis=1
    )
    piece = jnp.concatenate([piece, shift(piece, "zh", N_ZH, 1)], axis=0)

    texts[2], folded, far, inverse, piece = sync((texts[2], folded, far, inverse, piece))
    folded = place([folded, shift(folded, "c", N_C, 1)], c, 0)
    far = place([far, shift(far, "c", N_C, 1)], c, 0)
    normed = jnp.concatenate([normed_rows(value) for value in texts], axis=0)
    features = features[: N_Y * ROWS]
    flags = jnp.concatenate(
        [is_image(slot_order, ((y + r) % N_Y) * N_ZH + zh, slot[None]) for r in range(N_Y)]
    )
    part_a = place(ring(piece[:, :256], "x"), x, 1)
    own_y, after, across, before = ring(piece[:, 256:], "y")
    part_b = jnp.stack([own_y, before, across, after])

    blocks = project(flags, None, normed, features, inverse, own_weights, folded, 0)
    blocks = project(flags, blocks, normed, features, inverse, (far,), folded, 1)
    blocks, part_a, part_b = sync((blocks, part_a, part_b))
    blocks = blocks.reshape(SLOTS, ROWS, 3 * HEADSZ)
    own = lax.all_to_all(blocks, ("zl", "x"), split_axis=0, concat_axis=0, tiled=True)
    other = shift(own[:, :, HEADSZ:], "c", N_C, 1)
    own_y, after, across, before = ring(part_a, "y")
    part_a = jnp.stack([own_y, before, across, after])
    part_b = place(ring(part_b, "x"), x, 2)

    flags = is_image(slot_order, ((y + zl) % N_Y) * N_ZH + zh, jnp.arange(SLOTS))
    core = c[None].astype(jnp.int32)
    heads = attend(jnp.concatenate([flags, core]), own, other)

    heads, part_a, part_b = sync((heads, part_a, part_b))
    heads = lax.all_to_all(heads, ("zl", "x"), split_axis=0, concat_axis=0, tiled=True)
    heads = heads.reshape(N_Y, 4, ROWS, HEADSZ)
    merged = [heads[0]] + [shift(heads[r], "y", N_Y, N_Y - r) for r in range(1, N_Y)]
    far_a = shift(part_a, "c", N_C, 1)
    far_b = shift(part_b, "c", N_C, 1)
    return output(core, merged, (part_a, part_b, far_a, far_b))[None]


def attend_kernel(flags, own, other, out, scores):
    block = pl.program_id(0)
    core = flags[SLOTS]
    query = own[pl.ds(2 * block, 2), :, 0:128].reshape(256, 128)

    def chunk(ref, index, first):
        return ref[pl.ds(2 * index, 2), :, first : first + 128].reshape(256, 128)

    def dots(key):
        return lax.dot_general(
            query, key, (((1,), (1,)), ((), ())), preferred_element_type=jnp.float32
        )

    def halves(index):
        return dots(chunk(own, index, 128)), dots(chunk(other, index, 0))

    def top(value, mx):
        return jnp.maximum(mx, jnp.maximum(value[:, :128], value[:, 128:]))

    def first_pass(index, mx):
        mine, theirs = halves(index)
        start = pl.multiple_of(index * 512, 512)
        scores[:, pl.ds(start, 256)] = mine
        scores[:, pl.ds(start + 256, 256)] = theirs
        return top(theirs, top(mine, mx))

    mx = lax.fori_loop(0, block, first_pass, jnp.full((256, 128), -jnp.inf, jnp.float32))
    mine, theirs = halves(block)
    q_id = lax.broadcasted_iota(jnp.int32, (256, 256), 0)
    k_id = lax.broadcasted_iota(jnp.int32, (256, 256), 1)
    q_slot, k_slot = q_id // 128, k_id // 128
    image = jnp.where(q_slot == 0, flags[2 * block], flags[2 * block + 1]) > 0
    same = q_slot == k_slot
    earlier = k_slot < q_slot
    mine_ok = earlier | (same & ((k_id <= q_id) | image))
    theirs_ok = earlier | (same & (image | (core == 1)))
    mine = jnp.where(mine_ok, mine, -jnp.inf)
    theirs = jnp.where(theirs_ok, theirs, -jnp.inf)
    last = pl.multiple_of(block * 512, 512)
    scores[:, pl.ds(last, 256)] = mine
    scores[:, pl.ds(last + 256, 256)] = theirs
    mx = top(theirs, top(mine, mx))
    limit = jnp.max(mx, axis=1, keepdims=True) * EXP2_SCALE

    def second_pass(index, carry):
        total, acc = carry
        start = pl.multiple_of(index * 512, 512)
        mine = jnp.exp2(scores[:, pl.ds(start, 256)] * EXP2_SCALE - limit)
        theirs = jnp.exp2(scores[:, pl.ds(start + 256, 256)] * EXP2_SCALE - limit)
        total = total + (mine[:, :128] + mine[:, 128:]) + (theirs[:, :128] + theirs[:, 128:])
        acc = acc + jnp.dot(
            mine.astype(jnp.bfloat16), chunk(own, index, 256), preferred_element_type=jnp.float32
        )
        acc = acc + jnp.dot(
            theirs.astype(jnp.bfloat16), chunk(other, index, 128), preferred_element_type=jnp.float32
        )
        return total, acc

    zero = jnp.zeros((256, 128), jnp.float32)
    total, acc = lax.fori_loop(0, block + 1, second_pass, (zero, zero))
    total = jnp.sum(total, axis=1, keepdims=True)
    out[...] = (acc / total).astype(jnp.bfloat16).reshape(2, 128, 128)


def attend(flags, own, other):
    return pl.pallas_call(
        attend_kernel,
        out_shape=jax.ShapeDtypeStruct((SLOTS, ROWS, HEADSZ), jnp.bfloat16),
        grid_spec=pltpu.PrefetchScalarGridSpec(
            num_scalar_prefetch=1,
            grid=(SLOTS // 2,),
            in_specs=[
                pl.BlockSpec((SLOTS, ROWS, 3 * HEADSZ), lambda i, s: (0, 0, 0)),
                pl.BlockSpec((SLOTS, ROWS, 2 * HEADSZ), lambda i, s: (0, 0, 0)),
            ],
            out_specs=pl.BlockSpec((2, ROWS, HEADSZ), lambda i, s: (i, 0, 0)),
            scratch_shapes=[pltpu.VMEM((256, 4096), jnp.float32)],
        ),
        compiler_params=pltpu.CompilerParams(vmem_limit_bytes=32 * 1024 * 1024),
        cost_estimate=pl.CostEstimate(
            flops=4 * 36 * 256 * 512 * 128, bytes_accessed=3 << 20, transcendentals=36 * 256 * 512
        ),
    )(flags, own, other)


def solution(mesh):
    fine = Mesh(
        np.asarray(mesh.devices).reshape(N_Y, N_ZH, N_ZL, N_X, N_C), ("y", "zh", "zl", "x", "c")
    )
    dp, seq = ("y", "zh"), ("zl", "x", "c")
    return jax.shard_map(
        shards,
        mesh=fine,
        in_specs=(
            P(dp, seq, None),
            P(dp, seq, None),
            P(),
            P(),
            P(None, dp),
            P(),
            P(None, dp),
            P(None, dp),
            P(None, dp),
            P(dp, None),
        ),
        out_specs=P(dp, seq, None),
        check_vma=False,
    )
```

```python
import functools
import math

import jax
import jax.numpy as jnp
import numpy as np
from jax import lax
from jax.experimental import pallas as pl
from jax.experimental.pallas import tpu as pltpu
from jax.sharding import Mesh, PartitionSpec as P

HEADSZ = 128
LAT_SIDE = 32
LAT_C = 8
IMG_TOK = 256
N_Y, N_ZH, N_ZL, N_X, N_C = 4, 2, 4, 4, 2
ROWS = 128
SLOTS = 16
IMGS = 8
D = 4096
MICROSECOND = 1_150_000_000
MEBI = 1024 * 1024
EXP2_SCALE = HEADSZ**-0.5 * math.log2(math.e)


def shift(value, axis, size, step):
    return lax.ppermute(value, axis, [((i + step) % size, i) for i in range(size)])


def ring(value, axis):
    after = shift(value, axis, 4, 1)
    before = shift(value, axis, 4, 3)
    across = shift(value, axis, 4, 2)
    return [value, after, across, before]


def patch_matrix(conv_weight):
    taps = conv_weight.reshape(3, 3, LAT_C, -1)
    cells = [
        jnp.pad(taps, ((i, 1 - i), (j, 1 - j), (0, 0), (0, 0))) for i in range(2) for j in range(2)
    ]
    return jnp.stack(cells, axis=3).reshape(16 * LAT_C, -1)


def features_of(rows, conv_weight):
    count = rows.shape[0]
    padded = jnp.pad(rows, ((0, 0), (0, 0), (LAT_C, LAT_C)))
    pairs = padded.reshape(count, 18, 17, 2 * LAT_C)
    parts = []
    for row in range(4):
        line = pairs[:, row : row + 15 : 2]
        parts += [line[:, :, :16], line[:, :, 1:]]
    windows = jnp.concatenate(parts, axis=3).reshape(count * ROWS, 16 * LAT_C)
    feature = jnp.dot(
        windows, patch_matrix(conv_weight), preferred_element_type=jnp.float32
    )
    return jax.nn.silu(feature).astype(jnp.bfloat16)


def whole(shape):
    return pl.BlockSpec(shape, lambda i, s: (0,) * len(shape))


def pick_kernel(place, query, key, value, out):
    for part, ref in enumerate((query, key, value)):
        out[:, part * 256 : part * 256 + 256] = ref[...]


def pick(place, weights):
    return pl.pallas_call(
        pick_kernel,
        out_shape=jax.ShapeDtypeStruct((512, 768), jnp.bfloat16),
        grid_spec=pltpu.PrefetchScalarGridSpec(
            num_scalar_prefetch=1,
            grid=(1,),
            in_specs=[pl.BlockSpec((512, 256), lambda i, s: (s[0], 0))] * 3,
            out_specs=whole((512, 768)),
        ),
    )(place, *weights)


def fold_kernel(place, *refs):
    patches, gain, weights, out, total = refs[:4], refs[4], refs[5:8], refs[8], refs[9]
    step = pl.program_id(0)

    @pl.when(step == 0)
    def _():
        total[...] = jnp.zeros_like(total)

    for turn in range(N_Y):

        @pl.when(step // 2 == turn)
        def _(turn=turn):
            cols = pl.ds(pl.multiple_of((step % 2) * 512, 512), 512)
            rows = (patches[turn][0:128, cols].astype(jnp.float32) * gain[...]).astype(jnp.bfloat16)
            for part in range(3):
                total[:, part * 256 : part * 256 + 256] += jnp.dot(
                    rows, weights[part][...], preferred_element_type=jnp.float32
                )

    @pl.when(step == 7)
    def _():
        out[...] = total[...].astype(jnp.bfloat16)


def fold(place, patches, gain, weights):
    def block(i, s):
        return ((s[0] + i // 2) % N_Y) * 2 + (s[1] + i % 2) % 2

    return pl.pallas_call(
        fold_kernel,
        out_shape=jax.ShapeDtypeStruct((128, 768), jnp.bfloat16),
        grid_spec=pltpu.PrefetchScalarGridSpec(
            num_scalar_prefetch=1,
            grid=(8,),
            in_specs=[whole(patches[0].shape)] * 4
            + [pl.BlockSpec((1, 512), lambda i, s: (0, block(i, s)))]
            + [pl.BlockSpec((512, 256), lambda i, s: (block(i, s), 0))] * 3,
            out_specs=whole((128, 768)),
            scratch_shapes=[pltpu.VMEM((128, 768), jnp.float32)],
        ),
        compiler_params=pltpu.CompilerParams(vmem_limit_bytes=24 * MEBI),
        cost_estimate=pl.CostEstimate(
            flops=4 * MICROSECOND, bytes_accessed=8 << 20, transcendentals=0
        ),
    )(place, *patches, gain, *weights)


def place_heads(out, total, part):
    for seq in range(N_Y):
        kept = total[seq * ROWS : seq * ROWS + ROWS].astype(jnp.bfloat16)
        for head in range(2):
            out[seq, head, :, part * HEADSZ : part * HEADSZ + HEADSZ] = kept[
                :, head * HEADSZ : head * HEADSZ + HEADSZ
            ]


def copies(sems, pairs):
    started = []
    for number, (source, target) in enumerate(pairs):
        copy = pltpu.make_async_copy(source, target, sems.at[number])
        copy.start()
        started.append(copy)
    return started


def near_kernel(info, texts, query, key, value, out, rows, weights, sems):
    pairs = [
        (texts.at[(info[0] + seq) % N_Y], rows.at[pl.ds(seq * ROWS, ROWS)]) for seq in range(N_Y)
    ]
    pairs += [(ref, weights.at[part]) for part, ref in enumerate((query, key, value))]
    started = copies(sems, pairs)
    for copy in started[:N_Y]:
        copy.wait()
    for part in range(3):
        started[N_Y + part].wait()
        total = jnp.dot(rows[...], weights[part], preferred_element_type=jnp.float32)
        place_heads(out, total, part)


def far_kernel(info, texts, own, other, out, rows, weights, sems):
    core, column, ring_place = info[0], info[1], info[2]
    pairs = [(own, weights.at[0]), (other, weights.at[1])]
    for turn in range(8):
        first = (core + turn // 4) % 2 * 4 + (column + turn % 4) % 4
        first = pl.multiple_of(first * 512, 512)
        for seq in range(N_Y):
            pairs.append(
                (
                    texts.at[(ring_place + seq) % N_Y, :, pl.ds(first, 512)],
                    rows.at[pl.ds(seq * ROWS, ROWS), pl.ds(turn * 512, 512)],
                )
            )
    for copy in copies(sems, pairs):
        copy.wait()
    for part in range(3):
        total = jnp.zeros((N_Y * ROWS, 256), jnp.float32)
        for side in range(2):
            total = total + jnp.dot(
                rows[:, side * 2048 : side * 2048 + 2048],
                weights[side, :, :, part * 256 : part * 256 + 256].reshape(2048, 256),
                preferred_element_type=jnp.float32,
            )
        place_heads(out, total, part)


def image_kernel(info, near, far, features, inverse, own, other, out, parts, weights, sems):
    core, column = info[4], info[5]
    pairs = [(own, weights.at[0]), (other, weights.at[1])]
    for turn in range(8):
        first = (core + turn // 4) % 2 * 4 + (column + turn % 4) % 4
        first = pl.multiple_of(first * 128, 128)
        pairs.append(
            (
                features.at[pl.ds(0, N_Y * ROWS), pl.ds(first, 128)],
                parts.at[:, pl.ds(turn * 128, 128)],
            )
        )
    started = copies(sems, pairs)
    out[:, 0:2] = near[...]
    out[:, 2:4] = far[...]
    for copy in started:
        copy.wait()
    for part in range(6):
        total = jnp.zeros((N_Y * ROWS, 256), jnp.float32)
        for side in range(2):
            total = total + jnp.dot(
                parts[:, side * 512 : side * 512 + 512],
                weights[side, :, :, part * 256 : part * 256 + 256].reshape(512, 256),
                preferred_element_type=jnp.float32,
            )
        total = (total * inverse[...]).astype(jnp.bfloat16)
        cols = slice(part % 3 * HEADSZ, part % 3 * HEADSZ + HEADSZ)
        for seq in range(N_Y):

            @pl.when(info[seq] > 0)
            def _(seq=seq):
                for head in range(2):
                    out[seq, part // 3 * 2 + head, :, cols] = total[
                        seq * ROWS : seq * ROWS + ROWS, head * HEADSZ : head * HEADSZ + HEADSZ
                    ]


HBM = pl.BlockSpec(memory_space=pl.ANY)


def kernel_call(kernel, heads, info, args, in_specs, scratch, time, sems):
    shape = (N_Y, heads, ROWS, 3 * HEADSZ)
    return pl.pallas_call(
        kernel,
        out_shape=jax.ShapeDtypeStruct(shape, jnp.bfloat16),
        grid_spec=pltpu.PrefetchScalarGridSpec(
            num_scalar_prefetch=1,
            grid=(1,),
            in_specs=in_specs,
            out_specs=whole(shape),
            scratch_shapes=[pltpu.VMEM(size, jnp.bfloat16) for size in scratch]
            + [pltpu.SemaphoreType.DMA((sems,))],
        ),
        compiler_params=pltpu.CompilerParams(vmem_limit_bytes=40 * MEBI),
        cost_estimate=pl.CostEstimate(
            flops=time * MICROSECOND, bytes_accessed=12 << 20, transcendentals=0
        ),
    )(info, *args)


def project_near(info, texts, weights):
    return kernel_call(
        near_kernel, 2, info, (texts, *weights), [HBM] * 4, [(N_Y * ROWS, D), (3, D, 256)], 7, 7
    )


def project_far(info, texts, weights):
    return kernel_call(
        far_kernel, 2, info, (texts, *weights), [HBM] * 3,
        [(N_Y * ROWS, D), (2, 4, 512, 768)], 7, 34,
    )


def project_images(info, near, far, features, inverse, folded):
    return kernel_call(
        image_kernel, 4, info, (near, far, features, inverse, *folded),
        [whole(near.shape)] * 2 + [HBM, whole((N_Y * ROWS, 1)), HBM, HBM],
        [(N_Y * ROWS, 1024), (2, 4, 128, 1536)], 7, 10,
    )


def output_kernel(info, own, other, part, mine, theirs, rows):
    @pl.when(pl.program_id(0) == 0)
    def _():
        for core, heads in enumerate((own, other)):
            for step in range(N_Y):
                first = pl.multiple_of((info[1] + N_Y - step) % N_Y * 512, 512)
                for head in range(4):
                    rows[core * ROWS : core * ROWS + ROWS, pl.ds(first + head * HEADSZ, HEADSZ)] = (
                        heads[step, head]
                    )

    weight = part[...].reshape(2048, 512)
    total = jnp.dot(rows[...], weight, preferred_element_type=jnp.float32).astype(jnp.bfloat16)
    mine[...] = total[:ROWS]
    theirs[...] = total[ROWS:]


def output(info, own, other, part):
    return pl.pallas_call(
        output_kernel,
        out_shape=(
            jax.ShapeDtypeStruct((ROWS, D), jnp.bfloat16),
            jax.ShapeDtypeStruct((ROWS, D // 2), jnp.bfloat16),
        ),
        grid_spec=pltpu.PrefetchScalarGridSpec(
            num_scalar_prefetch=1,
            grid=(4,),
            in_specs=[whole((N_Y, 4, ROWS, HEADSZ))] * 2
            + [pl.BlockSpec((1, N_Y, 512, 512), lambda i, s: (i, 0, 0, 0))],
            out_specs=[
                pl.BlockSpec((ROWS, 512), lambda i, s: (0, 4 * s[0] + i)),
                pl.BlockSpec((ROWS, 512), lambda i, s: (0, i)),
            ],
            scratch_shapes=[pltpu.VMEM((2 * ROWS, 2048), jnp.bfloat16)],
        ),
        compiler_params=pltpu.CompilerParams(vmem_limit_bytes=60 * MEBI),
        cost_estimate=pl.CostEstimate(
            flops=7 * MICROSECOND, bytes_accessed=10 << 20, transcendentals=0
        ),
    )(info, own, other, part)


def attend_kernel(flags, own, other, out, scores):
    block = pl.program_id(0)
    core = flags[SLOTS]
    query = own[pl.ds(2 * block, 2), :, 0:128].reshape(256, 128)

    def chunk(ref, index, first):
        return ref[pl.ds(2 * index, 2), :, first : first + 128].reshape(256, 128)

    def dots(key):
        return lax.dot_general(
            query, key, (((1,), (1,)), ((), ())), preferred_element_type=jnp.float32
        )

    def halves(index):
        return dots(chunk(own, index, 128)), dots(chunk(other, index, 0))

    def top(value, mx):
        return jnp.maximum(mx, jnp.maximum(value[:, :128], value[:, 128:]))

    def first_pass(index, mx):
        mine, theirs = halves(index)
        start = pl.multiple_of(index * 512, 512)
        scores[:, pl.ds(start, 256)] = mine
        scores[:, pl.ds(start + 256, 256)] = theirs
        return top(theirs, top(mine, mx))

    mx = lax.fori_loop(0, block, first_pass, jnp.full((256, 128), -jnp.inf, jnp.float32))
    mine, theirs = halves(block)
    q_id = lax.broadcasted_iota(jnp.int32, (256, 256), 0)
    k_id = lax.broadcasted_iota(jnp.int32, (256, 256), 1)
    q_slot, k_slot = q_id // 128, k_id // 128
    image = jnp.where(q_slot == 0, flags[2 * block], flags[2 * block + 1]) > 0
    same = q_slot == k_slot
    earlier = k_slot < q_slot
    mine_ok = earlier | (same & ((k_id <= q_id) | image))
    theirs_ok = earlier | (same & (image | (core == 1)))
    mine = jnp.where(mine_ok, mine, -jnp.inf)
    theirs = jnp.where(theirs_ok, theirs, -jnp.inf)
    last = pl.multiple_of(block * 512, 512)
    scores[:, pl.ds(last, 256)] = mine
    scores[:, pl.ds(last + 256, 256)] = theirs
    mx = top(theirs, top(mine, mx))
    limit = jnp.max(mx, axis=1, keepdims=True) * EXP2_SCALE

    def second_pass(index, carry):
        total, acc = carry
        start = pl.multiple_of(index * 512, 512)
        mine = jnp.exp2(scores[:, pl.ds(start, 256)] * EXP2_SCALE - limit)
        theirs = jnp.exp2(scores[:, pl.ds(start + 256, 256)] * EXP2_SCALE - limit)
        total = total + (mine[:, :128] + mine[:, 128:]) + (theirs[:, :128] + theirs[:, 128:])
        acc = acc + jnp.dot(
            mine.astype(jnp.bfloat16), chunk(own, index, 256), preferred_element_type=jnp.float32
        )
        acc = acc + jnp.dot(
            theirs.astype(jnp.bfloat16), chunk(other, index, 128), preferred_element_type=jnp.float32
        )
        return total, acc

    zero = jnp.zeros((256, 128), jnp.float32)
    total, acc = lax.fori_loop(0, block + 1, second_pass, (zero, zero))
    total = jnp.sum(total, axis=1, keepdims=True)
    out[...] = (acc / total).astype(jnp.bfloat16).reshape(2, 128, 128)


def attend(flags, own, other):
    return pl.pallas_call(
        attend_kernel,
        out_shape=jax.ShapeDtypeStruct((SLOTS, ROWS, HEADSZ), jnp.bfloat16),
        grid_spec=pltpu.PrefetchScalarGridSpec(
            num_scalar_prefetch=1,
            grid=(SLOTS // 2,),
            in_specs=[
                pl.BlockSpec((SLOTS, ROWS, 3 * HEADSZ), lambda i, s: (0, 0, 0)),
                pl.BlockSpec((SLOTS, ROWS, 2 * HEADSZ), lambda i, s: (0, 0, 0)),
            ],
            out_specs=pl.BlockSpec((2, ROWS, HEADSZ), lambda i, s: (i, 0, 0)),
            scratch_shapes=[pltpu.VMEM((256, 4096), jnp.float32)],
        ),
        compiler_params=pltpu.CompilerParams(vmem_limit_bytes=32 * MEBI),
        cost_estimate=pl.CostEstimate(
            flops=20 * MICROSECOND, bytes_accessed=3 << 20, transcendentals=36 * 256 * 512
        ),
    )(flags, own, other)


def is_image(slot_order, seq, slot):
    row = lax.dynamic_slice_in_dim(slot_order, seq, 1, 0)[0]
    return jnp.any(row[None, :IMGS] == slot[:, None], axis=1).astype(jnp.int32)


def shards(
    text_embed,
    latents,
    slot_order,
    conv_weight,
    patch_weight,
    norm_gain,
    query_weight,
    key_weight,
    value_weight,
    out_weight,
):
    y, zh, zl, x, c = (lax.axis_index(name) for name in ("y", "zh", "zl", "x", "c"))
    slot = zl * N_X + x
    weights = (query_weight, key_weight, value_weight)
    sync = lax.optimization_barrier

    def scalars(*values):
        return jnp.stack(values).astype(jnp.int32)

    def swap(value, axis, size, bit):
        return lax.ppermute(value, axis, [(i, i ^ bit) for i in range(size)])

    def normalised(texts):
        widened = texts.astype(jnp.float32)
        scale = lax.rsqrt(jnp.mean(widened * widened, axis=2, keepdims=True) + 1e-05)
        return (widened * scale * norm_gain).astype(jnp.bfloat16)

    far = swap(pick(scalars(c * 4 + x), weights), "zh", N_ZH, 1)

    patches = lax.dynamic_slice_in_dim(patch_weight, (c * 4 + x) * 128, 128, 0)
    swapped = swap(patches, "zh", N_ZH, 1)
    spread = jnp.broadcast_to(latents, (N_ZL * N_X * N_C, 8, LAT_SIDE * LAT_C))
    lat_rows = lax.all_to_all(spread, ("zl", "x", "c"), split_axis=0, concat_axis=0, tiled=True)
    swapped, lat_rows = sync((swapped, lat_rows))

    lat_rows = lat_rows.reshape(-1, LAT_SIDE * LAT_C)
    slot_row = lax.dynamic_slice_in_dim(slot_order, y * N_ZH + zh, 1, 0)[0]
    image = jnp.sum(jnp.where(slot_row[:IMGS] == slot, jnp.arange(IMGS, dtype=jnp.int32), 0))
    first = (image * LAT_SIDE + c * 16 - 17) % (IMGS * LAT_SIDE)
    lat_rows = jnp.concatenate([lat_rows, lat_rows[:32]], axis=0)
    mine = lax.dynamic_slice_in_dim(lat_rows, first, 18, 0)
    row_id = jnp.arange(18)
    inside = ((row_id != 0) | (c != 0)) & ((row_id != 17) | (c != 1))
    mine = jnp.where(inside[:, None], mine, jnp.zeros_like(mine))
    patches = jnp.concatenate([patches, swapped], axis=1)
    patches = ring(jnp.concatenate([patches, jnp.pad(mine, ((0, 14), (0, 768)))]), "y")
    patches, far, out_weight, text_embed = sync((patches, far, out_weight, text_embed))

    texts = lax.all_gather(text_embed[0], "y", axis=0)

    far = ring(far, "x")
    images = jnp.stack([part[128:146, : LAT_SIDE * LAT_C] for part in patches])
    images = jnp.concatenate([images, swap(images, "zh", N_ZH, 1)])
    folded = fold(scalars(y, zh), patches, norm_gain[None], weights)
    folded = jnp.concatenate([folded, swap(folded, "zh", N_ZH, 1)], axis=1)
    piece = lax.dynamic_slice_in_dim(out_weight, (c * 4 + x) * 512, 512, 1)
    piece = jnp.concatenate([piece, swap(piece, "zh", N_ZH, 1)], axis=0)
    features = features_of(images, conv_weight)
    features, folded, far = sync((features, folded, far))
    embedded = jnp.dot(features, patch_weight, preferred_element_type=jnp.float32)
    squares = jnp.sum(embedded * embedded, axis=1).reshape(2, N_Y, ROWS)
    squares = squares[0] + swap(squares[1], "zh", N_ZH, 1)
    normed = normalised(texts)
    piece = lax.all_gather(piece, "y", axis=0)

    folded = ring(folded, "x")
    far = jnp.stack(far)
    far = [far, swap(far, "c", N_C, 1)]
    squares = jnp.roll(squares, y, axis=0)
    squares = squares + swap(squares, "y", N_Y, 1)
    squares = squares + swap(squares, "y", N_Y, 2)
    inverse = lax.rsqrt(jnp.roll(squares, -y, axis=0).reshape(N_Y * ROWS, 1) / D + 1e-05)
    near_blocks = project_near(scalars(y), normed, weights)
    near_blocks, folded, inverse = sync((near_blocks, folded, inverse))

    folded = jnp.stack(folded)
    folded = [folded, swap(folded, "c", N_C, 1)]
    flags = [is_image(slot_order, ((y + r) % N_Y) * N_ZH + zh, slot[None])[0] for r in range(N_Y)]
    far_blocks = project_far(scalars(c, x, y), normed, far)
    blocks = project_images(
        scalars(*flags, c, x), near_blocks, far_blocks, features, inverse, folded
    )

    blocks, piece = sync((blocks, piece))
    part = lax.all_gather(piece, "x", axis=0)
    blocks = blocks.reshape(SLOTS, ROWS, 3 * HEADSZ)
    own = lax.all_to_all(blocks, ("zl", "x"), split_axis=0, concat_axis=0, tiled=True)
    other = swap(own[:, :, HEADSZ:], "c", N_C, 1)

    flags = is_image(slot_order, ((y + zl) % N_Y) * N_ZH + zh, jnp.arange(SLOTS))
    heads = attend(jnp.concatenate([flags, scalars(c)]), own, other)

    heads = lax.all_to_all(heads, ("zl", "x"), split_axis=0, concat_axis=0, tiled=True)
    heads = heads.reshape(N_Y, 4, ROWS, HEADSZ)
    merged = [heads[0]] + [shift(heads[r], "y", N_Y, N_Y - r) for r in range(1, N_Y)]
    merged = jnp.stack(merged)
    result, theirs = output(scalars(c, y), merged, swap(merged, "c", N_C, 1), part)
    theirs = swap(theirs, "c", N_C, 1)
    return lax.dynamic_update_slice_in_dim(result, theirs, (1 - c) * (D // 2), 1)[None]


def solution(mesh):
    fine = Mesh(
        np.asarray(mesh.devices).reshape(N_Y, N_ZH, N_ZL, N_X, N_C), ("y", "zh", "zl", "x", "c")
    )
    dp, seq = ("y", "zh"), ("zl", "x", "c")
    return jax.shard_map(
        shards,
        mesh=fine,
        in_specs=(
            P(dp, seq, None),
            P(dp, seq, None),
            P(),
            P(),
            P(None, dp),
            P(),
            P(None, dp),
            P(None, dp),
            P(None, dp),
            P(dp, None),
        ),
        out_specs=P(dp, seq, None),
        check_vma=False,
    )
```

```python
import functools
import math

import jax
import jax.numpy as jnp
import numpy as np
from jax import lax
from jax.experimental import pallas as pl
from jax.experimental.pallas import tpu as pltpu
from jax.sharding import Mesh, PartitionSpec as P

HEADSZ = 128
LAT_SIDE = 32
LAT_C = 8
IMG_TOK = 256
N_Y, N_ZH, N_ZL, N_X, N_C = 4, 2, 4, 4, 2
ROWS = 128
SLOTS = 16
IMGS = 8
GROUP = 4
PLACE = 128
D = 4096
MICROSECOND = 1_150_000_000
MEBI = 1024 * 1024
EXP2_SCALE = HEADSZ**-0.5 * math.log2(math.e)


def shift(value, axis, size, step):
    return lax.ppermute(value, axis, [((i + step) % size, i) for i in range(size)])


def ring(value, axis):
    after = shift(value, axis, 4, 1)
    before = shift(value, axis, 4, 3)
    across = shift(value, axis, 4, 2)
    return [value, after, across, before]


def patch_matrix(conv_weight):
    taps = conv_weight.reshape(3, 3, LAT_C, -1)
    cells = [
        jnp.pad(taps, ((i, 1 - i), (j, 1 - j), (0, 0), (0, 0))) for i in range(2) for j in range(2)
    ]
    return jnp.stack(cells, axis=3).reshape(16 * LAT_C, -1)


def features_of(rows, conv_weight):
    count = rows.shape[0]
    padded = jnp.pad(rows, ((0, 0), (0, 0), (LAT_C, LAT_C)))
    pairs = padded.reshape(count, 18, 17, 2 * LAT_C)
    parts = []
    for row in range(4):
        line = pairs[:, row : row + 15 : 2]
        parts += [line[:, :, :16], line[:, :, 1:]]
    windows = jnp.concatenate(parts, axis=3).reshape(count * ROWS, 16 * LAT_C)
    feature = jnp.dot(
        windows, patch_matrix(conv_weight), preferred_element_type=jnp.float32
    )
    return jax.nn.silu(feature).astype(jnp.bfloat16)


def whole(shape):
    return pl.BlockSpec(shape, lambda i, s: (0,) * len(shape))


def pick_kernel(place, query, key, value, out):
    for part, ref in enumerate((query, key, value)):
        out[:, part * 256 : part * 256 + 256] = ref[...]


def pick(place, weights):
    return pl.pallas_call(
        pick_kernel,
        out_shape=jax.ShapeDtypeStruct((512, 768), jnp.bfloat16),
        grid_spec=pltpu.PrefetchScalarGridSpec(
            num_scalar_prefetch=1,
            grid=(1,),
            in_specs=[pl.BlockSpec((512, 256), lambda i, s: (s[PLACE + 4] * 4 + s[PLACE + 3], 0))] * 3,
            out_specs=whole((512, 768)),
        ),
    )(place, *weights)


def fold_kernel(place, *refs):
    patches, gain, weights, out, total = refs[:4], refs[4], refs[5:8], refs[8], refs[9]
    step = pl.program_id(0)

    @pl.when(step == 0)
    def _():
        total[...] = jnp.zeros_like(total)

    for turn in range(N_Y):

        @pl.when(step // 2 == turn)
        def _(turn=turn):
            cols = pl.ds(pl.multiple_of((step % 2) * 512, 512), 512)
            rows = (patches[turn][0:128, cols].astype(jnp.float32) * gain[...]).astype(jnp.bfloat16)
            for part in range(3):
                total[:, part * 256 : part * 256 + 256] += jnp.dot(
                    rows, weights[part][...], preferred_element_type=jnp.float32
                )

    @pl.when(step == 7)
    def _():
        out[...] = total[...].astype(jnp.bfloat16)


def fold(place, patches, gain, weights):
    def block(i, s):
        return ((s[PLACE] + i // 2) % N_Y) * 2 + (s[PLACE + 1] + i % 2) % 2

    return pl.pallas_call(
        fold_kernel,
        out_shape=jax.ShapeDtypeStruct((128, 768), jnp.bfloat16),
        grid_spec=pltpu.PrefetchScalarGridSpec(
            num_scalar_prefetch=1,
            grid=(8,),
            in_specs=[whole(patches[0].shape)] * 4
            + [pl.BlockSpec((1, 512), lambda i, s: (0, block(i, s)))]
            + [pl.BlockSpec((512, 256), lambda i, s: (block(i, s), 0))] * 3,
            out_specs=whole((128, 768)),
            scratch_shapes=[pltpu.VMEM((128, 768), jnp.float32)],
        ),
        compiler_params=pltpu.CompilerParams(vmem_limit_bytes=24 * MEBI),
        cost_estimate=pl.CostEstimate(
            flops=4 * MICROSECOND, bytes_accessed=8 << 20, transcendentals=0
        ),
    )(place, *patches, gain, *weights)


def held_at(info, step, slot):
    return info[((info[PLACE] + step) % N_Y * N_ZH + info[PLACE + 1]) * SLOTS + slot]


def place_heads(out, total, part):
    for seq in range(N_Y):
        kept = total[seq * ROWS : seq * ROWS + ROWS].astype(jnp.bfloat16)
        for head in range(2):
            out[seq, head, :, part * HEADSZ : part * HEADSZ + HEADSZ] = kept[
                :, head * HEADSZ : head * HEADSZ + HEADSZ
            ]


def copies(sems, pairs):
    started = []
    for number, (source, target) in enumerate(pairs):
        copy = pltpu.make_async_copy(source, target, sems.at[number])
        copy.start()
        started.append(copy)
    return started


def near_kernel(info, texts, query, key, value, out, rows, weights, sems):
    pairs = [
        (texts.at[(info[PLACE] + seq) % N_Y], rows.at[pl.ds(seq * ROWS, ROWS)]) for seq in range(N_Y)
    ]
    pairs += [(ref, weights.at[part]) for part, ref in enumerate((query, key, value))]
    started = copies(sems, pairs)
    for copy in started[:N_Y]:
        copy.wait()
    for part in range(3):
        started[N_Y + part].wait()
        total = jnp.dot(rows[...], weights[part], preferred_element_type=jnp.float32)
        place_heads(out, total, part)


def far_kernel(info, texts, own, other, out, rows, weights, sems):
    core, column, ring_place = info[PLACE + 4], info[PLACE + 3], info[PLACE]
    pairs = [(own, weights.at[0]), (other, weights.at[1])]
    for turn in range(8):
        first = (core + turn // 4) % 2 * 4 + (column + turn % 4) % 4
        first = pl.multiple_of(first * 512, 512)
        for seq in range(N_Y):
            pairs.append(
                (
                    texts.at[(ring_place + seq) % N_Y, :, pl.ds(first, 512)],
                    rows.at[pl.ds(seq * ROWS, ROWS), pl.ds(turn * 512, 512)],
                )
            )
    for copy in copies(sems, pairs):
        copy.wait()
    for part in range(3):
        total = jnp.zeros((N_Y * ROWS, 256), jnp.float32)
        for side in range(2):
            total = total + jnp.dot(
                rows[:, side * 2048 : side * 2048 + 2048],
                weights[side, :, :, part * 256 : part * 256 + 256].reshape(2048, 256),
                preferred_element_type=jnp.float32,
            )
        place_heads(out, total, part)


def image_kernel(info, near, far, features, inverse, own, other, out, parts, weights, sems):
    core, column = info[PLACE + 4], info[PLACE + 3]
    slot = info[PLACE + 2] * N_X + column
    pairs = [(own, weights.at[0]), (other, weights.at[1])]
    for turn in range(8):
        first = (core + turn // 4) % 2 * 4 + (column + turn % 4) % 4
        first = pl.multiple_of(first * 128, 128)
        pairs.append(
            (
                features.at[pl.ds(0, N_Y * ROWS), pl.ds(first, 128)],
                parts.at[:, pl.ds(turn * 128, 128)],
            )
        )
    started = copies(sems, pairs)
    out[:, 0:2] = near[...]
    out[:, 2:4] = far[...]
    for copy in started:
        copy.wait()
    for part in range(6):
        total = jnp.zeros((N_Y * ROWS, 256), jnp.float32)
        for side in range(2):
            total = total + jnp.dot(
                parts[:, side * 512 : side * 512 + 512],
                weights[side, :, :, part * 256 : part * 256 + 256].reshape(512, 256),
                preferred_element_type=jnp.float32,
            )
        total = (total * inverse[...]).astype(jnp.bfloat16)
        cols = slice(part % 3 * HEADSZ, part % 3 * HEADSZ + HEADSZ)
        for seq in range(N_Y):

            @pl.when(held_at(info, seq, slot) > 0)
            def _(seq=seq):
                for head in range(2):
                    out[seq, part // 3 * 2 + head, :, cols] = total[
                        seq * ROWS : seq * ROWS + ROWS, head * HEADSZ : head * HEADSZ + HEADSZ
                    ]


HBM = pl.BlockSpec(memory_space=pl.ANY)


def kernel_call(kernel, heads, info, args, in_specs, scratch, time, sems):
    shape = (N_Y, heads, ROWS, 3 * HEADSZ)
    return pl.pallas_call(
        kernel,
        out_shape=jax.ShapeDtypeStruct(shape, jnp.bfloat16),
        grid_spec=pltpu.PrefetchScalarGridSpec(
            num_scalar_prefetch=1,
            grid=(1,),
            in_specs=in_specs,
            out_specs=whole(shape),
            scratch_shapes=[pltpu.VMEM(size, jnp.bfloat16) for size in scratch]
            + [pltpu.SemaphoreType.DMA((sems,))],
        ),
        compiler_params=pltpu.CompilerParams(vmem_limit_bytes=40 * MEBI),
        cost_estimate=pl.CostEstimate(
            flops=time * MICROSECOND, bytes_accessed=12 << 20, transcendentals=0
        ),
    )(info, *args)


def project_near(info, texts, weights):
    return kernel_call(
        near_kernel, 2, info, (texts, *weights), [HBM] * 4, [(N_Y * ROWS, D), (3, D, 256)], 7, 7
    )


def project_far(info, texts, weights):
    return kernel_call(
        far_kernel, 2, info, (texts, *weights), [HBM] * 3,
        [(N_Y * ROWS, D), (2, 4, 512, 768)], 7, 34,
    )


def project_images(info, near, far, features, inverse, folded):
    return kernel_call(
        image_kernel, 4, info, (near, far, features, inverse, *folded),
        [whole(near.shape)] * 2 + [HBM, whole((N_Y * ROWS, 1)), HBM, HBM],
        [(N_Y * ROWS, 1024), (2, 4, 128, 1536)], 7, 10,
    )


def output_kernel(info, own, other, part, mine, theirs, rows):
    @pl.when(pl.program_id(0) == 0)
    def _():
        for core, heads in enumerate((own, other)):
            for step in range(N_Y):
                first = pl.multiple_of((info[PLACE] + N_Y - step) % N_Y * 512, 512)
                for head in range(4):
                    rows[core * ROWS : core * ROWS + ROWS, pl.ds(first + head * HEADSZ, HEADSZ)] = (
                        heads[step, head]
                    )

    weight = part[...].reshape(2048, 512)
    total = jnp.dot(rows[...], weight, preferred_element_type=jnp.float32).astype(jnp.bfloat16)
    mine[...] = total[:ROWS]
    theirs[...] = total[ROWS:]


def output(info, own, other, part):
    return pl.pallas_call(
        output_kernel,
        out_shape=(
            jax.ShapeDtypeStruct((ROWS, D), jnp.bfloat16),
            jax.ShapeDtypeStruct((ROWS, D // 2), jnp.bfloat16),
        ),
        grid_spec=pltpu.PrefetchScalarGridSpec(
            num_scalar_prefetch=1,
            grid=(4,),
            in_specs=[whole((N_Y, 4, ROWS, HEADSZ))] * 2
            + [pl.BlockSpec((1, N_Y, 512, 512), lambda i, s: (i, 0, 0, 0))],
            out_specs=[
                pl.BlockSpec((ROWS, 512), lambda i, s: (0, 4 * s[PLACE + 4] + i)),
                pl.BlockSpec((ROWS, 512), lambda i, s: (0, i)),
            ],
            scratch_shapes=[pltpu.VMEM((2 * ROWS, 2048), jnp.bfloat16)],
        ),
        compiler_params=pltpu.CompilerParams(vmem_limit_bytes=60 * MEBI),
        cost_estimate=pl.CostEstimate(
            flops=7 * MICROSECOND, bytes_accessed=10 << 20, transcendentals=0
        ),
    )(info, own, other, part)


def attend_kernel(info, own, other, out, scores):
    core, step = info[PLACE + 4], info[PLACE + 2]
    group = pl.program_id(0)
    rows = GROUP * ROWS
    query = own[pl.ds(GROUP * group, GROUP), :, 0:128].reshape(rows, 128)

    def chunk(ref, index, first):
        return ref[pl.ds(GROUP * index, GROUP), :, first : first + 128].reshape(rows, 128)

    def dots(key):
        return lax.dot_general(
            query, key, (((1,), (1,)), ((), ())), preferred_element_type=jnp.float32
        )

    def top(value, mx):
        for part in range(GROUP):
            mx = jnp.maximum(mx, value[:, part * 128 : part * 128 + 128])
        return mx

    def first_pass(index, mx):
        mine, theirs = dots(chunk(own, index, 128)), dots(chunk(other, index, 0))
        start = pl.multiple_of(index * 2 * rows, 2 * rows)
        scores[:, pl.ds(start, rows)] = mine
        scores[:, pl.ds(start + rows, rows)] = theirs
        return top(theirs, top(mine, mx))

    mx = lax.fori_loop(0, group, first_pass, jnp.full((rows, 128), -jnp.inf, jnp.float32))
    mine, theirs = dots(chunk(own, group, 128)), dots(chunk(other, group, 0))
    q_id = lax.broadcasted_iota(jnp.int32, (rows, rows), 0)
    k_id = lax.broadcasted_iota(jnp.int32, (rows, rows), 1)
    q_slot, k_slot = q_id // 128, k_id // 128
    image = jnp.zeros((rows, rows), jnp.bool_)
    for part in range(GROUP):
        held = held_at(info, step, GROUP * group + part) > 0
        image = image | ((q_slot == part) & held)
    same = q_slot == k_slot
    earlier = k_slot < q_slot
    mine_ok = earlier | (same & ((k_id <= q_id) | image))
    theirs_ok = earlier | (same & (image | (core == 1)))
    mine = jnp.where(mine_ok, mine, -jnp.inf)
    theirs = jnp.where(theirs_ok, theirs, -jnp.inf)
    last = pl.multiple_of(group * 2 * rows, 2 * rows)
    scores[:, pl.ds(last, rows)] = mine
    scores[:, pl.ds(last + rows, rows)] = theirs
    mx = top(theirs, top(mine, mx))
    limit = jnp.max(mx, axis=1, keepdims=True) * EXP2_SCALE

    def second_pass(index, carry):
        total, acc = carry
        start = pl.multiple_of(index * 2 * rows, 2 * rows)
        for half, ref, first in ((0, own, 256), (1, other, 128)):
            weight = jnp.exp2(scores[:, pl.ds(start + half * rows, rows)] * EXP2_SCALE - limit)
            value = jnp.concatenate([chunk(ref, index, first), jnp.ones((rows, 128), jnp.bfloat16)], axis=1)
            acc = acc + jnp.dot(
                weight.astype(jnp.bfloat16), value, preferred_element_type=jnp.float32
            )
        return total, acc

    zero = jnp.zeros((rows, 256), jnp.float32)
    _, acc = lax.fori_loop(0, group + 1, second_pass, (jnp.float32(0.0), zero))
    out[...] = (acc[:, :128] / acc[:, 128:]).astype(jnp.bfloat16).reshape(GROUP, ROWS, 128)


def attend(info, own, other):
    return pl.pallas_call(
        attend_kernel,
        out_shape=jax.ShapeDtypeStruct((SLOTS, ROWS, HEADSZ), jnp.bfloat16),
        grid_spec=pltpu.PrefetchScalarGridSpec(
            num_scalar_prefetch=1,
            grid=(SLOTS // GROUP,),
            in_specs=[
                pl.BlockSpec((SLOTS, ROWS, 3 * HEADSZ), lambda i, s: (0, 0, 0)),
                pl.BlockSpec((SLOTS, ROWS, 2 * HEADSZ), lambda i, s: (0, 0, 0)),
            ],
            out_specs=pl.BlockSpec((GROUP, ROWS, HEADSZ), lambda i, s: (i, 0, 0)),
            scratch_shapes=[pltpu.VMEM((GROUP * ROWS, 4096), jnp.float32)],
        ),
        compiler_params=pltpu.CompilerParams(vmem_limit_bytes=32 * MEBI),
        cost_estimate=pl.CostEstimate(
            flops=12 * MICROSECOND, bytes_accessed=3 << 20, transcendentals=36 * 256 * 512
        ),
    )(info, own, other)


def facts(slot_order, *place):
    held = slot_order[:, :IMGS, None] == jnp.arange(SLOTS, dtype=jnp.int32)
    held = jnp.any(held, axis=1).astype(jnp.int32).reshape(-1)
    return jnp.concatenate([held, jnp.stack(place).astype(jnp.int32)])


def shards(
    text_embed,
    latents,
    slot_order,
    conv_weight,
    patch_weight,
    norm_gain,
    query_weight,
    key_weight,
    value_weight,
    out_weight,
):
    y, zh, zl, x, c = (lax.axis_index(name) for name in ("y", "zh", "zl", "x", "c"))
    slot = zl * N_X + x
    weights = (query_weight, key_weight, value_weight)
    sync = lax.optimization_barrier
    info = facts(slot_order, y, zh, zl, x, c)

    def swap(value, axis, size, bit):
        return lax.ppermute(value, axis, [(i, i ^ bit) for i in range(size)])

    def normalised(texts):
        widened = texts.astype(jnp.float32)
        scale = lax.rsqrt(jnp.mean(widened * widened, axis=2, keepdims=True) + 1e-05)
        return (widened * scale * norm_gain).astype(jnp.bfloat16)

    far = swap(pick(info, weights), "zh", N_ZH, 1)

    patches = lax.dynamic_slice_in_dim(patch_weight, (c * 4 + x) * 128, 128, 0)
    swapped = swap(patches, "zh", N_ZH, 1)
    spread = jnp.broadcast_to(latents, (N_ZL * N_X * N_C, 8, LAT_SIDE * LAT_C))
    lat_rows = lax.all_to_all(spread, ("zl", "x", "c"), split_axis=0, concat_axis=0, tiled=True)
    swapped, lat_rows, text_embed = sync((swapped, lat_rows, text_embed))

    texts = lax.all_gather(text_embed[0], "y", axis=0)

    lat_rows = lat_rows.reshape(-1, LAT_SIDE * LAT_C)
    slot_row = lax.dynamic_slice_in_dim(slot_order, y * N_ZH + zh, 1, 0)[0]
    image = jnp.sum(jnp.where(slot_row[:IMGS] == slot, jnp.arange(IMGS, dtype=jnp.int32), 0))
    first = (image * LAT_SIDE + c * 16 - 17) % (IMGS * LAT_SIDE)
    lat_rows = jnp.concatenate([lat_rows, lat_rows[:32]], axis=0)
    mine = lax.dynamic_slice_in_dim(lat_rows, first, 18, 0)
    row_id = jnp.arange(18)
    inside = ((row_id != 0) | (c != 0)) & ((row_id != 17) | (c != 1))
    mine = jnp.where(inside[:, None], mine, jnp.zeros_like(mine))
    patches = jnp.concatenate([patches, swapped], axis=1)
    patches = ring(jnp.concatenate([patches, jnp.pad(mine, ((0, 14), (0, 768)))]), "y")
    patches, far, out_weight = sync((patches, far, out_weight))

    far = ring(far, "x")
    images = jnp.stack([part[128:146, : LAT_SIDE * LAT_C] for part in patches])
    images = jnp.concatenate([images, swap(images, "zh", N_ZH, 1)])
    folded = fold(info, patches, norm_gain[None], weights)
    folded = jnp.concatenate([folded, swap(folded, "zh", N_ZH, 1)], axis=1)
    piece = lax.dynamic_slice_in_dim(out_weight, (c * 4 + x) * 512, 512, 1)
    piece = jnp.concatenate([piece, swap(piece, "zh", N_ZH, 1)], axis=0)
    features = features_of(images, conv_weight)
    features, folded, far, piece = sync((features, folded, far, piece))
    piece = lax.all_gather(piece, "y", axis=0)
    embedded = jnp.dot(features, patch_weight, preferred_element_type=jnp.float32)
    squares = jnp.sum(embedded * embedded, axis=1).reshape(2, N_Y, ROWS)
    squares = squares[0] + swap(squares[1], "zh", N_ZH, 1)
    normed = normalised(texts)

    folded = ring(folded, "x")
    far = jnp.stack(far)
    far = [far, swap(far, "c", N_C, 1)]
    squares = jnp.roll(squares, y, axis=0)
    squares = squares + swap(squares, "y", N_Y, 1)
    squares = squares + swap(squares, "y", N_Y, 2)
    inverse = lax.rsqrt(jnp.roll(squares, -y, axis=0).reshape(N_Y * ROWS, 1) / D + 1e-05)
    near_blocks = project_near(info, normed, weights)
    near_blocks, folded, inverse, piece = sync((near_blocks, folded, inverse, piece))
    part = lax.all_gather(piece, "x", axis=0)

    folded = jnp.stack(folded)
    folded = [folded, swap(folded, "c", N_C, 1)]
    far_blocks = project_far(info, normed, far)
    blocks = project_images(
        info, near_blocks, far_blocks, features, inverse, folded
    )

    blocks = blocks.reshape(SLOTS, ROWS, 3 * HEADSZ)
    own = lax.all_to_all(blocks, ("zl", "x"), split_axis=0, concat_axis=0, tiled=True)
    other = swap(own[:, :, HEADSZ:], "c", N_C, 1)

    heads = attend(info, own, other)

    heads = lax.all_to_all(heads, ("zl", "x"), split_axis=0, concat_axis=0, tiled=True)
    heads = heads.reshape(N_Y, 4, ROWS, HEADSZ)
    merged = [heads[0]] + [shift(heads[r], "y", N_Y, N_Y - r) for r in range(1, N_Y)]
    merged = jnp.stack(merged)
    result, theirs = output(info, merged, swap(merged, "c", N_C, 1), part)
    theirs = swap(theirs, "c", N_C, 1)
    return lax.dynamic_update_slice_in_dim(result, theirs, (1 - c) * (D // 2), 1)[None]


def solution(mesh):
    fine = Mesh(
        np.asarray(mesh.devices).reshape(N_Y, N_ZH, N_ZL, N_X, N_C), ("y", "zh", "zl", "x", "c")
    )
    dp, seq = ("y", "zh"), ("zl", "x", "c")
    return jax.shard_map(
        shards,
        mesh=fine,
        in_specs=(
            P(dp, seq, None),
            P(dp, seq, None),
            P(),
            P(),
            P(None, dp),
            P(),
            P(None, dp),
            P(None, dp),
            P(None, dp),
            P(dp, None),
        ),
        out_specs=P(dp, seq, None),
        check_vma=False,
    )
```

```python
import functools
import math

import jax
import jax.numpy as jnp
import numpy as np
from jax import lax
from jax.experimental import pallas as pl
from jax.experimental.pallas import tpu as pltpu
from jax.sharding import Mesh, PartitionSpec as P

HEADSZ = 128
LAT_SIDE = 32
LAT_C = 8
IMG_TOK = 256
N_Y, N_ZH, N_ZL, N_X, N_C = 4, 2, 4, 4, 2
ROWS = 128
SLOTS = 16
IMGS = 8
GROUP = 4
PLACE = 128
D = 4096
MICROSECOND = 1_150_000_000
MEBI = 1024 * 1024
EXP2_SCALE = HEADSZ**-0.5 * math.log2(math.e)


def shift(value, axis, size, step):
    return lax.ppermute(value, axis, [((i + step) % size, i) for i in range(size)])


def ring(value, axis):
    after = shift(value, axis, 4, 1)
    before = shift(value, axis, 4, 3)
    across = shift(value, axis, 4, 2)
    return [value, after, across, before]


def patch_matrix(conv_weight):
    taps = conv_weight.reshape(3, 3, LAT_C, -1)
    cells = [
        jnp.pad(taps, ((i, 1 - i), (j, 1 - j), (0, 0), (0, 0))) for i in range(2) for j in range(2)
    ]
    return jnp.stack(cells, axis=3).reshape(16 * LAT_C, -1)


def features_of(rows, conv_weight):
    count = rows.shape[0]
    padded = jnp.pad(rows, ((0, 0), (0, 0), (LAT_C, LAT_C)))
    pairs = padded.reshape(count, 18, 17, 2 * LAT_C)
    parts = []
    for row in range(4):
        line = pairs[:, row : row + 15 : 2]
        parts += [line[:, :, :16], line[:, :, 1:]]
    windows = jnp.concatenate(parts, axis=3).reshape(count * ROWS, 16 * LAT_C)
    feature = jnp.dot(
        windows, patch_matrix(conv_weight), preferred_element_type=jnp.float32
    )
    return jax.nn.silu(feature).astype(jnp.bfloat16)


def whole(shape):
    return pl.BlockSpec(shape, lambda i, s: (0,) * len(shape))


def pick_kernel(place, query, key, value, out):
    for part, ref in enumerate((query, key, value)):
        out[:, part * 256 : part * 256 + 256] = ref[...]


def pick(place, weights):
    return pl.pallas_call(
        pick_kernel,
        out_shape=jax.ShapeDtypeStruct((512, 768), jnp.bfloat16),
        grid_spec=pltpu.PrefetchScalarGridSpec(
            num_scalar_prefetch=1,
            grid=(1,),
            in_specs=[pl.BlockSpec((512, 256), lambda i, s: (s[PLACE + 4] * 4 + s[PLACE + 3], 0))] * 3,
            out_specs=whole((512, 768)),
        ),
    )(place, *weights)


def fold_kernel(place, *refs):
    patches, gain, weights, out, total = refs[:4], refs[4], refs[5:8], refs[8], refs[9]
    step = pl.program_id(0)

    @pl.when(step == 0)
    def _():
        total[...] = jnp.zeros_like(total)

    for turn in range(N_Y):

        @pl.when(step // 2 == turn)
        def _(turn=turn):
            cols = pl.ds(pl.multiple_of((step % 2) * 512, 512), 512)
            rows = (patches[turn][0:128, cols].astype(jnp.float32) * gain[...]).astype(jnp.bfloat16)
            for part in range(3):
                total[:, part * 256 : part * 256 + 256] += jnp.dot(
                    rows, weights[part][...], preferred_element_type=jnp.float32
                )

    @pl.when(step == 7)
    def _():
        out[...] = total[...].astype(jnp.bfloat16)


def fold(place, patches, gain, weights):
    def block(i, s):
        return ((s[PLACE] + i // 2) % N_Y) * 2 + (s[PLACE + 1] + i % 2) % 2

    return pl.pallas_call(
        fold_kernel,
        out_shape=jax.ShapeDtypeStruct((128, 768), jnp.bfloat16),
        grid_spec=pltpu.PrefetchScalarGridSpec(
            num_scalar_prefetch=1,
            grid=(8,),
            in_specs=[whole(patches[0].shape)] * 4
            + [pl.BlockSpec((1, 512), lambda i, s: (0, block(i, s)))]
            + [pl.BlockSpec((512, 256), lambda i, s: (block(i, s), 0))] * 3,
            out_specs=whole((128, 768)),
            scratch_shapes=[pltpu.VMEM((128, 768), jnp.float32)],
        ),
        compiler_params=pltpu.CompilerParams(vmem_limit_bytes=24 * MEBI),
        cost_estimate=pl.CostEstimate(
            flops=4 * MICROSECOND, bytes_accessed=8 << 20, transcendentals=0
        ),
    )(place, *patches, gain, *weights)


def held_at(info, step, slot):
    return info[((info[PLACE] + step) % N_Y * N_ZH + info[PLACE + 1]) * SLOTS + slot]


def place_heads(out, total, part):
    for seq in range(N_Y):
        kept = total[seq * ROWS : seq * ROWS + ROWS].astype(jnp.bfloat16)
        for head in range(2):
            out[seq, head, :, part * HEADSZ : part * HEADSZ + HEADSZ] = kept[
                :, head * HEADSZ : head * HEADSZ + HEADSZ
            ]


def copies(sems, pairs):
    started = []
    for number, (source, target) in enumerate(pairs):
        copy = pltpu.make_async_copy(source, target, sems.at[number])
        copy.start()
        started.append(copy)
    return started


def near_kernel(info, texts, query, key, value, out, rows, weights, sems):
    pairs = [
        (texts.at[(info[PLACE] + seq) % N_Y], rows.at[pl.ds(seq * ROWS, ROWS)]) for seq in range(N_Y)
    ]
    pairs += [(ref, weights.at[part]) for part, ref in enumerate((query, key, value))]
    started = copies(sems, pairs)
    for copy in started[:N_Y]:
        copy.wait()
    for part in range(3):
        started[N_Y + part].wait()
        total = jnp.dot(rows[...], weights[part], preferred_element_type=jnp.float32)
        place_heads(out, total, part)


def far_kernel(info, texts, own, other, out, rows, weights, sems):
    core, column, ring_place = info[PLACE + 4], info[PLACE + 3], info[PLACE]
    pairs = [(own, weights.at[0]), (other, weights.at[1])]
    for turn in range(8):
        first = (core + turn // 4) % 2 * 4 + (column + turn % 4) % 4
        first = pl.multiple_of(first * 512, 512)
        for seq in range(N_Y):
            pairs.append(
                (
                    texts.at[(ring_place + seq) % N_Y, :, pl.ds(first, 512)],
                    rows.at[pl.ds(seq * ROWS, ROWS), pl.ds(turn * 512, 512)],
                )
            )
    for copy in copies(sems, pairs):
        copy.wait()
    for part in range(3):
        total = jnp.zeros((N_Y * ROWS, 256), jnp.float32)
        for side in range(2):
            total = total + jnp.dot(
                rows[:, side * 2048 : side * 2048 + 2048],
                weights[side, :, :, part * 256 : part * 256 + 256].reshape(2048, 256),
                preferred_element_type=jnp.float32,
            )
        place_heads(out, total, part)


def image_kernel(info, near, far, features, inverse, own, other, out, parts, weights, sems):
    core, column = info[PLACE + 4], info[PLACE + 3]
    slot = info[PLACE + 2] * N_X + column
    pairs = [(own, weights.at[0]), (other, weights.at[1])]
    for turn in range(8):
        first = (core + turn // 4) % 2 * 4 + (column + turn % 4) % 4
        first = pl.multiple_of(first * 128, 128)
        pairs.append(
            (
                features.at[pl.ds(0, N_Y * ROWS), pl.ds(first, 128)],
                parts.at[:, pl.ds(turn * 128, 128)],
            )
        )
    started = copies(sems, pairs)
    out[:, 0:2] = near[...]
    out[:, 2:4] = far[...]
    for copy in started:
        copy.wait()
    for part in range(6):
        total = jnp.zeros((N_Y * ROWS, 256), jnp.float32)
        for side in range(2):
            total = total + jnp.dot(
                parts[:, side * 512 : side * 512 + 512],
                weights[side, :, :, part * 256 : part * 256 + 256].reshape(512, 256),
                preferred_element_type=jnp.float32,
            )
        total = (total * inverse[...]).astype(jnp.bfloat16)
        cols = slice(part % 3 * HEADSZ, part % 3 * HEADSZ + HEADSZ)
        for seq in range(N_Y):

            @pl.when(held_at(info, seq, slot) > 0)
            def _(seq=seq):
                for head in range(2):
                    out[seq, part // 3 * 2 + head, :, cols] = total[
                        seq * ROWS : seq * ROWS + ROWS, head * HEADSZ : head * HEADSZ + HEADSZ
                    ]


HBM = pl.BlockSpec(memory_space=pl.ANY)


def kernel_call(kernel, heads, info, args, in_specs, scratch, time, sems):
    shape = (N_Y, heads, ROWS, 3 * HEADSZ)
    return pl.pallas_call(
        kernel,
        out_shape=jax.ShapeDtypeStruct(shape, jnp.bfloat16),
        grid_spec=pltpu.PrefetchScalarGridSpec(
            num_scalar_prefetch=1,
            grid=(1,),
            in_specs=in_specs,
            out_specs=whole(shape),
            scratch_shapes=[pltpu.VMEM(size, jnp.bfloat16) for size in scratch]
            + [pltpu.SemaphoreType.DMA((sems,))],
        ),
        compiler_params=pltpu.CompilerParams(vmem_limit_bytes=40 * MEBI),
        cost_estimate=pl.CostEstimate(
            flops=time * MICROSECOND, bytes_accessed=12 << 20, transcendentals=0
        ),
    )(info, *args)


def project_near(info, texts, weights):
    return kernel_call(
        near_kernel, 2, info, (texts, *weights), [HBM] * 4, [(N_Y * ROWS, D), (3, D, 256)], 7, 7
    )


def project_far(info, texts, weights):
    return kernel_call(
        far_kernel, 2, info, (texts, *weights), [HBM] * 3,
        [(N_Y * ROWS, D), (2, 4, 512, 768)], 7, 34,
    )


def project_images(info, near, far, features, inverse, folded):
    return kernel_call(
        image_kernel, 4, info, (near, far, features, inverse, *folded),
        [whole(near.shape)] * 2 + [HBM, whole((N_Y * ROWS, 1)), HBM, HBM],
        [(N_Y * ROWS, 1024), (2, 4, 128, 1536)], 7, 10,
    )


def output_kernel(info, own, other, part, mine, theirs, rows):
    @pl.when(pl.program_id(0) == 0)
    def _():
        for core, heads in enumerate((own, other)):
            for step in range(N_Y):
                first = pl.multiple_of((info[PLACE] + N_Y - step) % N_Y * 512, 512)
                for head in range(4):
                    rows[core * ROWS : core * ROWS + ROWS, pl.ds(first + head * HEADSZ, HEADSZ)] = (
                        heads[step, head]
                    )

    weight = part[...].reshape(2048, 512)
    total = jnp.dot(rows[...], weight, preferred_element_type=jnp.float32).astype(jnp.bfloat16)
    mine[...] = total[:ROWS]
    theirs[...] = total[ROWS:]


def output(info, own, other, part):
    return pl.pallas_call(
        output_kernel,
        out_shape=(
            jax.ShapeDtypeStruct((ROWS, D), jnp.bfloat16),
            jax.ShapeDtypeStruct((ROWS, D // 2), jnp.bfloat16),
        ),
        grid_spec=pltpu.PrefetchScalarGridSpec(
            num_scalar_prefetch=1,
            grid=(4,),
            in_specs=[whole((N_Y, 4, ROWS, HEADSZ))] * 2
            + [pl.BlockSpec((1, N_Y, 512, 512), lambda i, s: (i, 0, 0, 0))],
            out_specs=[
                pl.BlockSpec((ROWS, 512), lambda i, s: (0, 4 * s[PLACE + 4] + i)),
                pl.BlockSpec((ROWS, 512), lambda i, s: (0, i)),
            ],
            scratch_shapes=[pltpu.VMEM((2 * ROWS, 2048), jnp.bfloat16)],
        ),
        compiler_params=pltpu.CompilerParams(vmem_limit_bytes=60 * MEBI),
        cost_estimate=pl.CostEstimate(
            flops=7 * MICROSECOND, bytes_accessed=10 << 20, transcendentals=0
        ),
    )(info, own, other, part)


def attend_kernel(info, own, other, out, scores):
    core, step = info[PLACE + 4], info[PLACE + 2]
    group = pl.program_id(0)
    rows = GROUP * ROWS
    query = own[pl.ds(GROUP * group, GROUP), :, 0:128].reshape(rows, 128)

    def chunk(ref, index, first):
        return ref[pl.ds(GROUP * index, GROUP), :, first : first + 128].reshape(rows, 128)

    def dots(key):
        return lax.dot_general(
            query, key, (((1,), (1,)), ((), ())), preferred_element_type=jnp.float32
        )

    def top(value, mx):
        for part in range(GROUP):
            mx = jnp.maximum(mx, value[:, part * 128 : part * 128 + 128])
        return mx

    def first_pass(index, mx):
        mine, theirs = dots(chunk(own, index, 128)), dots(chunk(other, index, 0))
        start = pl.multiple_of(index * 2 * rows, 2 * rows)
        scores[:, pl.ds(start, rows)] = mine
        scores[:, pl.ds(start + rows, rows)] = theirs
        return top(theirs, top(mine, mx))

    mx = lax.fori_loop(0, group, first_pass, jnp.full((rows, 128), -jnp.inf, jnp.float32))
    mine, theirs = dots(chunk(own, group, 128)), dots(chunk(other, group, 0))
    q_id = lax.broadcasted_iota(jnp.int32, (rows, rows), 0)
    k_id = lax.broadcasted_iota(jnp.int32, (rows, rows), 1)
    q_slot, k_slot = q_id // 128, k_id // 128
    image = jnp.zeros((rows, rows), jnp.bool_)
    for part in range(GROUP):
        held = held_at(info, step, GROUP * group + part) > 0
        image = image | ((q_slot == part) & held)
    same = q_slot == k_slot
    earlier = k_slot < q_slot
    mine_ok = earlier | (same & ((k_id <= q_id) | image))
    theirs_ok = earlier | (same & (image | (core == 1)))
    mine = jnp.where(mine_ok, mine, -jnp.inf)
    theirs = jnp.where(theirs_ok, theirs, -jnp.inf)
    last = pl.multiple_of(group * 2 * rows, 2 * rows)
    scores[:, pl.ds(last, rows)] = mine
    scores[:, pl.ds(last + rows, rows)] = theirs
    mx = top(theirs, top(mine, mx))
    limit = jnp.max(mx, axis=1, keepdims=True) * EXP2_SCALE

    def second_pass(index, carry):
        total, acc = carry
        start = pl.multiple_of(index * 2 * rows, 2 * rows)
        for half, ref, first in ((0, own, 256), (1, other, 128)):
            weight = jnp.exp2(scores[:, pl.ds(start + half * rows, rows)] * EXP2_SCALE - limit)
            value = jnp.concatenate([chunk(ref, index, first), jnp.ones((rows, 128), jnp.bfloat16)], axis=1)
            acc = acc + jnp.dot(
                weight.astype(jnp.bfloat16), value, preferred_element_type=jnp.float32
            )
        return total, acc

    zero = jnp.zeros((rows, 256), jnp.float32)
    _, acc = lax.fori_loop(0, group + 1, second_pass, (jnp.float32(0.0), zero))
    out[...] = (acc[:, :128] / acc[:, 128:]).astype(jnp.bfloat16).reshape(GROUP, ROWS, 128)


def attend(info, own, other):
    return pl.pallas_call(
        attend_kernel,
        out_shape=jax.ShapeDtypeStruct((SLOTS, ROWS, HEADSZ), jnp.bfloat16),
        grid_spec=pltpu.PrefetchScalarGridSpec(
            num_scalar_prefetch=1,
            grid=(SLOTS // GROUP,),
            in_specs=[
                pl.BlockSpec((SLOTS, ROWS, 3 * HEADSZ), lambda i, s: (0, 0, 0)),
                pl.BlockSpec((SLOTS, ROWS, 2 * HEADSZ), lambda i, s: (0, 0, 0)),
            ],
            out_specs=pl.BlockSpec((GROUP, ROWS, HEADSZ), lambda i, s: (i, 0, 0)),
            scratch_shapes=[pltpu.VMEM((GROUP * ROWS, 4096), jnp.float32)],
        ),
        compiler_params=pltpu.CompilerParams(vmem_limit_bytes=32 * MEBI),
        cost_estimate=pl.CostEstimate(
            flops=12 * MICROSECOND, bytes_accessed=3 << 20, transcendentals=36 * 256 * 512
        ),
    )(info, own, other)


def facts(slot_order, *place):
    held = slot_order[:, :IMGS, None] == jnp.arange(SLOTS, dtype=jnp.int32)
    held = jnp.any(held, axis=1).astype(jnp.int32).reshape(-1)
    return jnp.concatenate([held, jnp.stack(place).astype(jnp.int32)])


def shards(
    text_embed,
    latents,
    slot_order,
    conv_weight,
    patch_weight,
    norm_gain,
    query_weight,
    key_weight,
    value_weight,
    out_weight,
):
    y, zh, zl, x, c = (lax.axis_index(name) for name in ("y", "zh", "zl", "x", "c"))
    slot = zl * N_X + x
    weights = (query_weight, key_weight, value_weight)
    sync = lax.optimization_barrier
    info = facts(slot_order, y, zh, zl, x, c)

    def swap(value, axis, size, bit):
        return lax.ppermute(value, axis, [(i, i ^ bit) for i in range(size)])

    def normalised(texts):
        widened = texts.astype(jnp.float32)
        scale = lax.rsqrt(jnp.mean(widened * widened, axis=2, keepdims=True) + 1e-05)
        return (widened * scale * norm_gain).astype(jnp.bfloat16)

    far = swap(pick(info, weights), "zh", N_ZH, 1)

    patches = lax.dynamic_slice_in_dim(patch_weight, (c * 4 + x) * 128, 128, 0)
    swapped = swap(patches, "zh", N_ZH, 1)
    spread = jnp.broadcast_to(latents, (N_ZL * N_X * N_C, 8, LAT_SIDE * LAT_C))
    lat_rows = lax.all_to_all(spread, ("zl", "x", "c"), split_axis=0, concat_axis=0, tiled=True)
    swapped, lat_rows, text_embed = sync((swapped, lat_rows, text_embed))

    texts = lax.all_gather(text_embed[0], "y", axis=0)

    lat_rows = lat_rows.reshape(-1, LAT_SIDE * LAT_C)
    slot_row = lax.dynamic_slice_in_dim(slot_order, y * N_ZH + zh, 1, 0)[0]
    image = jnp.sum(jnp.where(slot_row[:IMGS] == slot, jnp.arange(IMGS, dtype=jnp.int32), 0))
    first = (image * LAT_SIDE + c * 16 - 17) % (IMGS * LAT_SIDE)
    lat_rows = jnp.concatenate([lat_rows, lat_rows[:32]], axis=0)
    mine = lax.dynamic_slice_in_dim(lat_rows, first, 18, 0)
    row_id = jnp.arange(18)
    inside = ((row_id != 0) | (c != 0)) & ((row_id != 17) | (c != 1))
    mine = jnp.where(inside[:, None], mine, jnp.zeros_like(mine))
    patches = jnp.concatenate([patches, swapped], axis=1)
    patches = ring(jnp.concatenate([patches, jnp.pad(mine, ((0, 14), (0, 768)))]), "y")
    patches, far, out_weight = sync((patches, far, out_weight))

    far = ring(far, "x")
    images = jnp.stack([part[128:146, : LAT_SIDE * LAT_C] for part in patches])
    images = jnp.concatenate([images, swap(images, "zh", N_ZH, 1)])
    folded = fold(info, patches, norm_gain[None], weights)
    folded = jnp.concatenate([folded, swap(folded, "zh", N_ZH, 1)], axis=1)
    piece = lax.dynamic_slice_in_dim(out_weight, (c * 4 + x) * 512, 512, 1)
    piece = jnp.concatenate([piece, swap(piece, "zh", N_ZH, 1)], axis=0)
    features = features_of(images, conv_weight)
    features, folded, far, piece = sync((features, folded, far, piece))
    piece = lax.all_gather(piece, "y", axis=0)
    embedded = jnp.dot(features, patch_weight, preferred_element_type=jnp.float32)
    squares = jnp.sum(embedded * embedded, axis=1).reshape(2, N_Y, ROWS)
    squares = squares[0] + swap(squares[1], "zh", N_ZH, 1)
    normed = normalised(texts)

    folded = ring(folded, "x")
    far = jnp.stack(far)
    far = [far, swap(far, "c", N_C, 1)]
    squares = jnp.roll(squares, y, axis=0)
    squares = squares + swap(squares, "y", N_Y, 1)
    squares = squares + swap(squares, "y", N_Y, 2)
    inverse = lax.rsqrt(jnp.roll(squares, -y, axis=0).reshape(N_Y * ROWS, 1) / D + 1e-05)
    near_blocks = project_near(info, normed, weights)
    near_blocks, folded, piece = sync((near_blocks, folded, piece))
    part = lax.all_gather(piece, "x", axis=0)

    folded = jnp.stack(folded)
    folded = [folded, swap(folded, "c", N_C, 1)]
    far_blocks = project_far(info, normed, far)
    blocks = project_images(
        info, near_blocks, far_blocks, features, inverse, folded
    )

    blocks = blocks.reshape(SLOTS, ROWS, 3 * HEADSZ)
    own = lax.all_to_all(blocks, ("zl", "x"), split_axis=0, concat_axis=0, tiled=True)
    other = swap(own[:, :, HEADSZ:], "c", N_C, 1)

    heads = attend(info, own, other)

    heads = lax.all_to_all(heads, ("zl", "x"), split_axis=0, concat_axis=0, tiled=True)
    heads = heads.reshape(N_Y, 4, ROWS, HEADSZ)
    merged = [heads[0]] + [shift(heads[r], "y", N_Y, N_Y - r) for r in range(1, N_Y)]
    merged = jnp.stack(merged)
    result, theirs = output(info, merged, swap(merged, "c", N_C, 1), part)
    theirs = swap(theirs, "c", N_C, 1)
    return lax.dynamic_update_slice_in_dim(result, theirs, (1 - c) * (D // 2), 1)[None]


def solution(mesh):
    fine = Mesh(
        np.asarray(mesh.devices).reshape(N_Y, N_ZH, N_ZL, N_X, N_C), ("y", "zh", "zl", "x", "c")
    )
    dp, seq = ("y", "zh"), ("zl", "x", "c")
    return jax.shard_map(
        shards,
        mesh=fine,
        in_specs=(
            P(dp, seq, None),
            P(dp, seq, None),
            P(),
            P(),
            P(None, dp),
            P(),
            P(None, dp),
            P(None, dp),
            P(None, dp),
            P(dp, None),
        ),
        out_specs=P(dp, seq, None),
        check_vma=False,
    )
```
